32 devices in a mesh: groups: 2 (over y), wide: 4 (over z), narrow: 2 (over x), sub: 2 (over core).
Axes of the slice: x: 2, y: 2, z: 4, core: 2. Of those that a mesh axis runs over, the one named last changes fastest.
Arguments:
- state_vel: float32 [2, 512, 512], P(None, ('groups', 'wide'), 'narrow'), parts along dimension 1, may hold values from -6 to 6
- friction: float32 [512, 512], P(('groups', 'wide'), 'narrow'), parts along dimension 0, may hold values from -3 to 3
- basal_area: float32 [512, 512], P(('groups', 'wide'), 'narrow'), parts along dimension 0, may hold values from 0.5 to 2
- direction_beta: float32 [512, 512], P(('groups', 'wide'), 'narrow'), parts along dimension 0, may hold values from -6 to 6
- elem_nodes: int32 [3, 196608], P(None, ('groups', 'wide', 'narrow', 'sub')), parts along dimension 1, may hold values from 0 to 17027
- elem_geom: float32 [7, 196608], P(None, ('groups', 'wide', 'narrow', 'sub')), parts along dimension 1, as said below
- elem_thick: float32 [196608], P(('groups', 'wide', 'narrow', 'sub')), parts along dimension 0, may hold values from 0.3 to 3
- live_blocks: int32 [32], P(('groups', 'wide', 'narrow')), parts along dimension 0, may hold values from 16 to 48, as said below
- pix_dest: int32 [65536, 1], P(('groups', 'wide', 'narrow', 'sub')), parts along dimension 0, may hold values from 0 to 7; in each aligned block of 2048 rows (0 to 2047, 2048 to 4095, ...) at most 512 rows name the same one
- pix_prec: float32 [65536], P(('groups', 'wide', 'narrow', 'sub')), parts along dimension 0, may hold values from 1 to 10
- pix_couple: float32 [65536], P(('groups', 'wide', 'narrow', 'sub')), parts along dimension 0, may hold values from 0 to 0.45
- obs_nodes: int32 [3, 131072], P(None, ('groups', 'wide', 'narrow', 'sub')), parts along dimension 1, may hold values from 0 to 17027
- obs_bary: float32 [3, 131072], P(None, ('groups', 'wide', 'narrow', 'sub')), parts along dimension 1, may hold values from 0 to 1
- obs_angle: float32 [131072], P(('groups', 'wide', 'narrow', 'sub')), parts along dimension 0, may hold values from -3.140625 to 3.140625
Outputs:
- tangent_vel: float32 [2, 512, 512], P(None, ('groups', 'wide'), 'narrow'), parts along dimension 1
- hess_vec: float32 [512, 512], P(('groups', 'wide'), 'narrow'), parts along dimension 0
The draws below stay inside these ranges and needn't reach their ends.
There are 2 independent parts, one for each index of `groups`. The reference program is written for one: setup_inputs(seed, part) draws one part's arguments, and reference() takes and returns one part's arrays. A program takes and returns all parts, laid end to end along the dimension named above; each array names one. Nothing has to cross between parts.
Inputs may be any that keep to these rules, and one draw needn't show every extreme that they name: `live_blocks`: each device's live blocks are its first ones; the two cores of a partition hold at most 64 live blocks together; both bounds are reached. `pix_dest`: at most 512 pixels of one device have the same owner, reached. `elem_nodes`: index into the partition's node grid padded by one row and column on each side, row-major over (66) x (258). `obs_nodes`: as elem_nodes, in the owner partition. `elem_geom`: the three gradients of each direction sum to zero; the area is positive.
All inputs are finite; a program needn't handle non-finite values.
Results may differ from the reference program's by a relative error of at most 0.0003.
Values sent between devices are 32-bit elements; how exact they have to be, the bound alone decides.
A program may use at most 128 MiB of HBM per device.

```python
import math
import jax
import jax.numpy as jnp
import numpy as np
from jax import lax

RW = 64
CN = 256
EB = 48
PIX_DEV = 2048
CG_ITERS = 2
CAP = 512
ROWS = 256
COLS = 512
CORES = 16
ELEMS = 98304
PIXELS = 32768
SLOTS = 65536
N_WIDE = 4
N_NARROW = 2
N_SUB = 2


def draw_elem_geom(key, part):
    key = jax.random.fold_in(key, 11)
    grad_key, area_key = jax.random.split(key)
    gradients = jax.random.normal(grad_key, (4, ELEMS), jnp.float32)
    area = jnp.exp(jax.random.uniform(area_key, (1, ELEMS), jnp.float32, math.log(0.5), math.log(2.0)))
    third_x = -(gradients[0] + gradients[1])
    third_y = -(gradients[2] + gradients[3])
    return jnp.concatenate([gradients[0:2], third_x[None, :], gradients[2:4], third_y[None, :], area], axis=0)


def draw_live_blocks(key, part):
    key = jax.random.fold_in(key, 23)
    busy_key, forced_key, light_key, flip_key = jax.random.split(key, 4)
    pairs = N_WIDE * N_NARROW
    third = EB // 3
    busy = jax.random.randint(busy_key, (pairs,), third, EB + 1)
    forced = jax.random.randint(forced_key, (), 0, pairs)
    busy = jnp.where(jnp.arange(pairs) == forced, EB, busy)
    light = jax.random.randint(light_key, (pairs,), third, 4 * third - busy + 1)
    flip = jax.random.randint(flip_key, (pairs,), 0, 2)
    first = jnp.where(flip == 1, busy, light)
    second = jnp.where(flip == 1, light, busy)
    return jnp.stack([first, second], axis=1).reshape(-1).astype(jnp.int32)


def place_ends(result, key, low, high):
    shape = result.shape
    spot = [jax.random.randint(jax.random.fold_in(key, axis), (), 0, shape[axis]) for axis in range(len(shape))]
    result = result.at[tuple(spot)].set(low)
    longest = shape.index(max(shape))
    spot[longest] = (spot[longest] + 1) % shape[longest]
    return result.at[tuple(spot)].set(high)


def steps_of(rng, shape, cuts, least, high):
    def one(axis_at, parts):
        steps = jax.random.uniform(jax.random.fold_in(jax.random.fold_in(rng, 6), axis_at), (parts,), jnp.float32, least / len(cuts), high / len(cuts))
        return jnp.repeat(jnp.exp(steps), shape[axis_at] // parts).reshape((-1,) + (1,) * (len(shape) - axis_at - 1))

    factor_of = one(*cuts[0])
    for cut in cuts[1:]:
        factor_of = factor_of * one(*cut)
    return factor_of


def routed_block(stream_key, own, number, rows, number_of, top, reach, slope):
    ranking = jax.random.permutation(stream_key, number_of)
    crowded, usual = load_shares(number_of, rows * top, reach, slope, True), load_shares(number_of, rows * top, reach, slope, False)
    places = jnp.arange(number_of)

    def named(sizes, rotation):
        used = int((sizes > 0).sum())
        fixed = max(1, used // 4)
        moved = fixed + (places - fixed + rotation * (used - fixed)) % max(1, number_of - fixed)
        return jnp.zeros((number_of,), jnp.int32).at[ranking[jnp.where(places < fixed, places, moved)]].set(jnp.asarray(sizes, jnp.int32))

    sizes = jnp.where(number % 4 == 0, named(crowded, number // 4), named(usual, number - number // 4 - 1))
    mixed = jax.random.permutation(jax.random.fold_in(own, 3), number_of)
    source_of, receiver = mixed[0:number_of // 2 * 2:2], mixed[1:number_of // 2 * 2:2]
    margin = jnp.minimum(sizes[source_of] - 1, reach - sizes[receiver]) // 2
    margin = jnp.where((source_of == ranking[0]) | (receiver == ranking[0]) | (sizes[receiver] == 0), 0, jnp.maximum(margin, 0))
    moved = jax.random.randint(jax.random.fold_in(own, 4), (number_of // 2,), 0, 1 << 20) % (margin + 1)
    sizes = sizes.at[source_of].add(-moved).at[receiver].add(moved)
    members = jnp.searchsorted(jnp.cumsum(sizes), jnp.arange(rows * top), side="right").astype(jnp.int32)
    grid = members.reshape(top, rows).T
    grid = grid[jax.random.permutation(jax.random.fold_in(own, 1), rows)]
    rotation = jax.random.randint(jax.random.fold_in(own, 2), (rows, 1), 0, top)
    return jnp.take_along_axis(grid, (jnp.arange(top)[None, :] + rotation) % top, axis=1)


def load_shares(amount, total, reach, slope, full):
    portions = [(1 << 20) // math.isqrt(standing ** slope) + 1 for standing in range(1, amount + 1)]
    largest = reach if full else min(reach, max(-(-total // amount), total * portions[0] // sum(portions)))
    least = 1 if total - largest >= amount - 1 else 0
    holding, spare = [largest] + [least] * (amount - 1), total - largest - least * (amount - 1)
    while spare > 0:
        free = [i for i in range(1, amount) if holding[i] < largest] or [i for i in range(1, amount) if holding[i] < reach]
        whole, remaining = sum([portions[i] for i in free]), spare
        for i in free:
            more = min(reach - holding[i], max(1, remaining * portions[i] // whole), spare)
            holding[i] = holding[i] + more
            spare = spare - more
    return np.array(holding)


def gaussian(key, dims, deviation, limit, shards=(), held_as=jnp.bfloat16):
    values = jax.random.normal(key, dims, jnp.float32) * deviation
    if len(shards) > 0:
        values = steps_of(key, dims, shards, -0.22, 0.18) * values
    return jnp.clip(values, min=-limit, max=limit).astype(held_as)


def setup_inputs(seed: int = 0, part: int = 0) -> dict:
    seeds = jax.random.split(jax.random.key(seed), 15)
    part_splits = jax.random.split(jax.random.fold_in(seeds[14], part), 15)
    state_vel = gaussian(part_splits[0], (2, ROWS, COLS), 1.0, 6.0, ((1, 4), (2, 2)), jnp.float32)
    friction = gaussian(part_splits[1], (ROWS, COLS), 0.5, 3.0, ((0, 4), (1, 2)), jnp.float32)
    basal_area = jnp.clip(jnp.exp(math.log(2.0) - 1.3862944 * jax.random.uniform(part_splits[2], (ROWS, COLS), jnp.float32) ** steps_of(part_splits[2], (ROWS, COLS), ((0, 4), (1, 2)), -0.2, 0.2)), 0.5, 2.0)
    direction_beta = gaussian(part_splits[3], (ROWS, COLS), 1.0, 6.0, ((0, 4), (1, 2)), jnp.float32)
    elem_nodes = place_ends(jax.random.randint(part_splits[4], (3, ELEMS), 0, (RW + 2) * (CN + 2)), jax.random.fold_in(part_splits[4], 1), 0, ((RW + 2) * (CN + 2)) - 1).astype(jnp.int32)
    elem_geom = draw_elem_geom(jax.random.fold_in(jax.random.fold_in(seeds[14], part), 71), part)
    elem_thick = jnp.clip(jnp.exp(math.log(3.0) - 2.3025851 * jax.random.uniform(part_splits[6], (ELEMS,), jnp.float32) ** steps_of(part_splits[6], (ELEMS,), ((0, 16),), -0.2, 0.2)), 0.3, 3.0)
    live_blocks = draw_live_blocks(jax.random.fold_in(jax.random.fold_in(seeds[14], part), 71), part)
    pix_dest_keys = jax.random.split(jax.random.fold_in(part_splits[8], 1), PIXELS // PIX_DEV)
    pix_dest_turns = jax.random.permutation(jax.random.fold_in(part_splits[8], 3), PIXELS // PIX_DEV)
    pix_dest = jax.vmap(lambda own, number: routed_block(jax.random.fold_in(part_splits[8], 2), own, number, PIX_DEV, N_WIDE * N_NARROW, 1, CAP, 2))(pix_dest_keys, pix_dest_turns).reshape((PIXELS, 1))
    pix_prec = jnp.clip(jnp.exp(math.log(10.0) - 2.3025851 * jax.random.uniform(part_splits[9], (PIXELS,), jnp.float32) ** steps_of(part_splits[9], (PIXELS,), ((0, 16),), -0.2, 0.2)), 1.0, 10.0)
    pix_couple = jnp.clip(0.45 * jax.random.uniform(part_splits[10], (PIXELS,), jnp.float32) ** steps_of(part_splits[10], (PIXELS,), ((0, 16),), -0.2, 0.2), 0.0, 0.45)
    obs_nodes = place_ends(jax.random.randint(part_splits[11], (3, SLOTS), 0, (RW + 2) * (CN + 2)), jax.random.fold_in(part_splits[11], 1), 0, ((RW + 2) * (CN + 2)) - 1).astype(jnp.int32)
    obs_bary = jnp.clip(1.0 * jax.random.uniform(part_splits[12], (3, SLOTS), jnp.float32) ** steps_of(part_splits[12], (3, SLOTS), ((1, 16),), -0.2, 0.2), 0.0, 1.0)
    obs_angle = jnp.clip(jax.random.uniform(part_splits[13], (SLOTS,), jnp.float32, -3.140625, 3.140625), -3.140625, 3.140625)
    return {"state_vel": state_vel, "friction": friction, "basal_area": basal_area, "direction_beta": direction_beta, "elem_nodes": elem_nodes, "elem_geom": elem_geom, "elem_thick": elem_thick, "live_blocks": live_blocks, "pix_dest": pix_dest, "pix_prec": pix_prec, "pix_couple": pix_couple, "obs_nodes": obs_nodes, "obs_bary": obs_bary, "obs_angle": obs_angle}


GLEN_B = 1.0
STRAIN_FLOOR = 0.01

def strains(values, geometry):
    strain_xx = lax.optimization_barrier(jnp.sum(geometry[0:3] * values[0], axis=0))
    strain_yy = lax.optimization_barrier(jnp.sum(geometry[3:6] * values[1], axis=0))
    strain_xy = 0.5 * lax.optimization_barrier(jnp.sum(geometry[3:6] * values[0] + geometry[0:3] * values[1], axis=0))
    return (strain_xx, strain_yy, strain_xy)

def forces(values, geometry, coefficient):
    strain_xx, strain_yy, strain_xy = strains(values, geometry)
    stress_xx = coefficient * (2.0 * strain_xx + strain_yy)
    stress_yy = coefficient * (strain_xx + 2.0 * strain_yy)
    stress_xy = coefficient * strain_xy
    force_x = stress_xx * geometry[0:3] + stress_xy * geometry[3:6]
    force_y = stress_yy * geometry[3:6] + stress_xy * geometry[0:3]
    return (force_x, force_y)

def weigh_rows(readings, precision, couple):
    grid_read = readings.reshape(-1, 128)
    grid_prec = precision.reshape(-1, 128)
    grid_couple = couple.reshape(-1, 128)
    column = jnp.arange(128)[None, :]
    next_prec = jnp.concatenate([grid_prec[:, 1:], grid_prec[:, :1]], axis=1)
    link_weight = jnp.where(column < 127, grid_couple * jnp.sqrt(grid_prec * next_prec), 0.0)
    zero_col = jnp.zeros_like(grid_read[:, :1])
    next_read = jnp.concatenate([grid_read[:, 1:], zero_col], axis=1)
    prev_read = jnp.concatenate([zero_col, grid_read[:, :-1]], axis=1)
    prev_link = jnp.concatenate([zero_col, link_weight[:, :-1]], axis=1)
    return (grid_prec * grid_read - link_weight * next_read - prev_link * prev_read).reshape(-1)

def global_index(local_ids, device):
    partition = device // N_SUB
    wide_pos = partition // N_NARROW
    narrow_pos = partition % N_NARROW
    row_pos = local_ids // (CN + 2) + wide_pos * RW
    col_pos = local_ids % (CN + 2) + narrow_pos * CN
    return (row_pos * (COLS + 2) + col_pos).astype(jnp.int32)

def reference(state_vel, friction, basal_area, direction_beta, elem_nodes, elem_geom, elem_thick, live_blocks, pix_dest, pix_prec, pix_couple, obs_nodes, obs_bary, obs_angle):
    padded_count = (ROWS + 2) * (COLS + 2)
    owners = N_WIDE * N_NARROW
    elem_index = jnp.arange(ELEMS, dtype=jnp.int32)
    elem_device = elem_index // (EB * 128)
    elem_block = elem_index % (EB * 128) // 128
    live_mask = (elem_block < live_blocks[elem_device]).astype(jnp.float32)
    vertex_ids = global_index(elem_nodes, elem_device[None, :])
    basal_drag = jnp.exp(friction) * basal_area

    def ghosted(field):
        return jnp.pad(field, ((0, 0), (1, 1), (1, 1))).reshape(2, padded_count)

    def assemble(force_x, force_y, targets):
        flat_ids = targets.reshape(-1)
        sum_x = jax.ops.segment_sum(force_x.reshape(-1), flat_ids, padded_count)
        sum_y = jax.ops.segment_sum(force_y.reshape(-1), flat_ids, padded_count)
        return jnp.stack([sum_x, sum_y]).reshape(2, ROWS + 2, COLS + 2)[:, 1:-1, 1:-1]
    state_values = ghosted(state_vel)[:, vertex_ids]
    strain_xx, strain_yy, strain_xy = strains(state_values, elem_geom)
    effective = strain_xx * strain_xx + strain_yy * strain_yy + strain_xx * strain_yy + strain_xy * strain_xy + STRAIN_FLOOR
    viscosity = 0.5 * GLEN_B * effective ** (-1.0 / 3.0)
    coefficient = 2.0 * viscosity * elem_thick * elem_geom[6] * live_mask

    def operate(field):
        values = ghosted(field)[:, vertex_ids]
        force_x, force_y = forces(values, elem_geom, coefficient)
        return assemble(force_x, force_y, vertex_ids) + basal_drag * field

    def solve_field(right_side):
        solution = jnp.zeros_like(right_side)
        residual = right_side
        direction = right_side
        norm_now = jnp.sum(residual * residual)
        for iteration in range(CG_ITERS):
            applied = operate(direction)
            step_size = norm_now / jnp.sum(direction * applied)
            solution = solution + step_size * direction
            residual = residual - step_size * applied
            if iteration + 1 < CG_ITERS:
                norm_next = jnp.sum(residual * residual)
                direction = residual + norm_next / norm_now * direction
                norm_now = norm_next
        return solution

    def row_ranks(target):
        onehot = (target[:, None] == jnp.arange(owners, dtype=jnp.int32)[None, :]).astype(jnp.int32)
        running = jnp.cumsum(onehot, axis=0, dtype=jnp.int32)
        return jnp.take_along_axis(running, target[:, None], axis=1)[:, 0] - 1
    target_all = pix_dest[:, 0]
    slot_rank = lax.map(row_ranks, target_all.reshape(CORES, PIX_DEV)).reshape(-1).astype(jnp.int32)
    source = jnp.arange(PIXELS, dtype=jnp.int32) // PIX_DEV
    owner_device = target_all * N_SUB + source % N_SUB
    table = (owner_device * (owners * CAP) + source // N_SUB * CAP + slot_rank).astype(jnp.int32)
    table_nodes = global_index(obs_nodes[:, table], owner_device[None, :])
    table_bary = obs_bary[:, table]
    cosine = jnp.cos(obs_angle[table])
    sine = jnp.sin(obs_angle[table])
    tangent_vel = solve_field(-basal_drag * direction_beta * state_vel)
    picked = ghosted(tangent_vel)[:, table_nodes]
    readings = lax.optimization_barrier(jnp.sum(table_bary * (cosine * picked[0] + sine * picked[1]), axis=0))
    weighted = weigh_rows(readings, pix_prec, pix_couple)
    adjoint_rhs = assemble(table_bary * weighted * cosine, table_bary * weighted * sine, table_nodes)
    adjoint = solve_field(adjoint_rhs)
    hess_vec = -basal_drag * (state_vel[0] * adjoint[0] + state_vel[1] * adjoint[1])
    return (tangent_vel, hess_vec)
```

```python
import functools

import jax
import jax.numpy as jnp
from jax import lax
from jax.experimental import pallas as pl
from jax.experimental.pallas import tpu as pltpu
from jax.sharding import PartitionSpec as P

CG_ITERS = 2

GLEN_B = 1.0
STRAIN_FLOOR = 0.01
RIM = 128
CHUNK = 512


def padded(block, sides, width):
    for axis, dim in sides:
        count = lax.axis_size(axis)
        forward = [(i, i + 1) for i in range(count - 1)]
        backward = [(target, source) for source, target in forward]
        low = lax.ppermute(
            lax.slice_in_dim(block, block.shape[dim] - width, None, axis=dim), axis, forward
        )
        high = lax.ppermute(lax.slice_in_dim(block, 0, width, axis=dim), axis, backward)
        block = jnp.concatenate([low, block, high], axis=dim)
    return block


def split_pair(values):
    high = values.astype(jnp.bfloat16)
    low = (values - high.astype(jnp.float32)).astype(jnp.bfloat16)
    return high, low


def stack_field(field):
    high_x, low_x = split_pair(field[0])
    high_y, low_y = split_pair(field[1])
    return jnp.concatenate([high_x, high_y, low_x, low_y], axis=0)


def column_onehot(low_ids, width):
    place = lax.broadcasted_iota(jnp.int32, (width, low_ids.shape[1]), 0)
    return jnp.where(place == low_ids, 1.0, 0.0).astype(jnp.bfloat16)


def row_mask(high_ids, rows):
    return lax.broadcasted_iota(jnp.int32, (rows, high_ids.shape[1]), 0) == high_ids


def pick(stacked, mask, onehot):
    rows = mask.shape[0]
    grown = jnp.dot(stacked, onehot, preferred_element_type=jnp.float32)
    both = grown[: 2 * rows] + grown[2 * rows :]
    value_x = jnp.sum(jnp.where(mask, both[:rows], 0.0), axis=0, keepdims=True)
    value_y = jnp.sum(jnp.where(mask, both[rows:], 0.0), axis=0, keepdims=True)
    return value_x, value_y


def masked_stack(mask, value_x, value_y):
    parts = split_f32(value_x, value_y)
    return jnp.concatenate(
        [jnp.where(mask, part, 0.0).astype(jnp.bfloat16) for part in parts], axis=0
    )


def split_f32(value_x, value_y):
    high_x = value_x.astype(jnp.bfloat16).astype(jnp.float32)
    high_y = value_y.astype(jnp.bfloat16).astype(jnp.float32)
    return high_x, high_y, value_x - high_x, value_y - high_y


def add_in(stacks, onehots):
    left = jnp.concatenate(stacks, axis=1)
    right = jnp.concatenate(onehots, axis=1)
    return lax.dot_general(
        left, right, (((1,), (1,)), ((), ())), preferred_element_type=jnp.float32
    )


def unstack(total):
    both = total[: total.shape[0] // 2] + total[total.shape[0] // 2 :]
    rows = both.shape[0] // 2
    return both[:rows], both[rows:]


def strain_rows(values, grad):
    value_x, value_y = values
    strain_xx = grad[0] * value_x[0] + grad[1] * value_x[1] + grad[2] * value_x[2]
    strain_yy = grad[3] * value_y[0] + grad[4] * value_y[1] + grad[5] * value_y[2]
    strain_xy = 0.5 * (
        (grad[3] * value_x[0] + grad[0] * value_y[0])
        + (grad[4] * value_x[1] + grad[1] * value_y[1])
        + (grad[5] * value_x[2] + grad[2] * value_y[2])
    )
    return strain_xx, strain_yy, strain_xy


def chunk_of(step):
    return pl.ds(pl.multiple_of(step * CHUNK, CHUNK), CHUNK)


def gather_chunk(stacked, high_ref, low_ref, cols, rows, width):
    masks, onehots, value_x, value_y = [], [], [], []
    for a in range(3):
        mask = row_mask(high_ref[a : a + 1, cols], rows)
        onehot = column_onehot(low_ref[a : a + 1, cols], width)
        got_x, got_y = pick(stacked, mask, onehot)
        masks.append(mask)
        onehots.append(onehot)
        value_x.append(got_x)
        value_y.append(got_y)
    return masks, onehots, (value_x, value_y)


def viscosity_loop(stack_ref, high_ref, low_ref, geom_ref, scale_ref, coef_ref, rows):
    width = stack_ref.shape[1]

    def body(step, carry):
        cols = chunk_of(step)
        _, _, values = gather_chunk(stack_ref[...], high_ref, low_ref, cols, rows, width)
        grad = [geom_ref[i : i + 1, cols] for i in range(6)]
        exx, eyy, exy = strain_rows(values, grad)
        effective = exx * exx + eyy * eyy + exx * eyy + exy * exy + STRAIN_FLOOR
        viscosity = 0.5 * GLEN_B * jnp.exp(jnp.log(effective) * (-1.0 / 3.0))
        coef_ref[:, cols] = 2.0 * viscosity * scale_ref[:, cols]
        return carry

    lax.fori_loop(0, high_ref.shape[1] // CHUNK, body, 0)


def operate_loop(stack_ref, high_ref, low_ref, geom_ref, coef_ref, total_ref, rows):
    width = stack_ref.shape[1]
    total_ref[...] = jnp.zeros_like(total_ref)

    def body(step, carry):
        cols = chunk_of(step)
        masks, onehots, values = gather_chunk(
            stack_ref[...], high_ref, low_ref, cols, rows, width
        )
        grad = [geom_ref[i : i + 1, cols] for i in range(6)]
        coefficient = coef_ref[:, cols]
        exx, eyy, exy = strain_rows(values, grad)
        sxx = coefficient * (2.0 * exx + eyy)
        syy = coefficient * (exx + 2.0 * eyy)
        sxy = coefficient * exy
        stacks = [
            masked_stack(
                masks[a],
                sxx * grad[a] + sxy * grad[3 + a],
                syy * grad[3 + a] + sxy * grad[a],
            )
            for a in range(3)
        ]
        total_ref[...] += add_in(stacks, onehots)
        return carry

    lax.fori_loop(0, high_ref.shape[1] // CHUNK, body, 0)


def read_loop(stack_ref, high_ref, low_ref, weight_x_ref, weight_y_ref, read_ref, rows):
    width = stack_ref.shape[1]

    def body(step, carry):
        cols = chunk_of(step)
        _, _, values = gather_chunk(stack_ref[...], high_ref, low_ref, cols, rows, width)
        total = 0.0
        for a in range(3):
            total = total + (
                weight_x_ref[a : a + 1, cols] * values[0][a]
                + weight_y_ref[a : a + 1, cols] * values[1][a]
            )
        read_ref[:, cols] = total
        return carry

    lax.fori_loop(0, high_ref.shape[1] // CHUNK, body, 0)


def spread_loop(arrived_ref, high_ref, low_ref, weight_x_ref, weight_y_ref, total_ref, rows):
    width = total_ref.shape[1]
    total_ref[...] = jnp.zeros_like(total_ref)

    def body(step, carry):
        cols = chunk_of(step)
        arrived = arrived_ref[:, cols]
        stacks, onehots = [], []
        for a in range(3):
            mask = row_mask(high_ref[a : a + 1, cols], rows)
            onehots.append(column_onehot(low_ref[a : a + 1, cols], width))
            stacks.append(
                masked_stack(
                    mask,
                    arrived * weight_x_ref[a : a + 1, cols],
                    arrived * weight_y_ref[a : a + 1, cols],
                )
            )
        total_ref[...] += add_in(stacks, onehots)
        return carry

    lax.fori_loop(0, high_ref.shape[1] // CHUNK, body, 0)


def viscosity_kernel(field_ref, high_ref, low_ref, geom_ref, scale_ref, coef_ref, stack_ref):
    stack_ref[...] = stack_field(field_ref)
    viscosity_loop(
        stack_ref, high_ref, low_ref, geom_ref, scale_ref, coef_ref, field_ref.shape[1]
    )


def operate_kernel(
    field_ref, high_ref, low_ref, geom_ref, coef_ref, out_ref, stack_ref, total_ref
):
    stack_ref[...] = stack_field(field_ref)
    operate_loop(
        stack_ref, high_ref, low_ref, geom_ref, coef_ref, total_ref, field_ref.shape[1]
    )
    out_ref[0], out_ref[1] = unstack(total_ref[...])


def read_kernel(field_ref, high_ref, low_ref, wx_ref, wy_ref, read_ref, stack_ref):
    stack_ref[...] = stack_field(field_ref)
    read_loop(stack_ref, high_ref, low_ref, wx_ref, wy_ref, read_ref, field_ref.shape[1])


def spread_kernel(arrived_ref, high_ref, low_ref, wx_ref, wy_ref, out_ref, total_ref):
    spread_loop(arrived_ref, high_ref, low_ref, wx_ref, wy_ref, total_ref, out_ref.shape[1])
    out_ref[0], out_ref[1] = unstack(total_ref[...])


def call(kernel, out, scratch, *args):
    return pl.pallas_call(
        kernel,
        out_shape=jax.ShapeDtypeStruct(out, jnp.float32),
        in_specs=[pl.BlockSpec(memory_space=pltpu.VMEM)] * len(args),
        out_specs=pl.BlockSpec(memory_space=pltpu.VMEM),
        scratch_shapes=scratch,
        compiler_params=pltpu.CompilerParams(vmem_limit_bytes=48 * 1024 * 1024),
    )(*args)


def split_ids(ids, node_rows, columns):
    row = ids // (columns + 2)
    col = ids % (columns + 2)
    left, right = col == 0, col == columns + 1
    high = jnp.where(left | right, node_rows + 2, row)
    low = jnp.where(left, row, jnp.where(right, row + RIM, col - 1))
    return high, low


def weigh_rows(readings, precision, couple):
    grid_read = readings.reshape(-1, 128)
    grid_prec = precision.reshape(-1, 128)
    grid_couple = couple.reshape(-1, 128)
    column = jnp.arange(128)[None, :]
    next_prec = jnp.concatenate([grid_prec[:, 1:], grid_prec[:, :1]], axis=1)
    link_weight = jnp.where(column < 127, grid_couple * jnp.sqrt(grid_prec * next_prec), 0.0)
    zero_col = jnp.zeros_like(grid_read[:, :1])
    next_read = jnp.concatenate([grid_read[:, 1:], zero_col], axis=1)
    prev_read = jnp.concatenate([zero_col, grid_read[:, :-1]], axis=1)
    prev_link = jnp.concatenate([zero_col, link_weight[:, :-1]], axis=1)
    return (grid_prec * grid_read - link_weight * next_read - prev_link * prev_read).reshape(-1)


def ghosted(field):
    return padded(field, (("wide", 1), ("narrow", 2)), 1)


def reduce_rims(summed):
    side_cols = jnp.concatenate([summed[:, :, :1], summed[:, :, -1:]], axis=2)
    beside = padded(side_cols, (("narrow", 2),), 1)
    middle = summed[:, :, 1:-1]
    middle = middle.at[:, :, 0].add(beside[:, :, 0]).at[:, :, -1].add(beside[:, :, 3])
    side_rows = jnp.concatenate([middle[:, :1], middle[:, -1:]], axis=1)
    across = padded(side_rows, (("wide", 1),), 1)
    interior = middle[:, 1:-1]
    return interior.at[:, 0].add(across[:, 0]).at[:, -1].add(across[:, 3])


def norm_sum(residual):
    return lax.psum(jnp.sum(residual * residual), ("wide", "narrow"))


def per_device(
    state_vel,
    friction,
    basal_area,
    direction_beta,
    elem_nodes,
    elem_geom,
    elem_thick,
    live_blocks,
    pix_dest,
    pix_prec,
    pix_couple,
    obs_nodes,
    obs_bary,
    obs_angle,
):
    node_rows, columns = friction.shape
    rows = -(-(node_rows + 3) // 8) * 8
    elements = elem_nodes.shape[1]
    core_index = lax.axis_index("sub")
    alive = jnp.arange(elements, dtype=jnp.int32) // 128 < live_blocks[core_index]
    scale = jnp.where(alive, elem_thick * elem_geom[6], 0.0)[None, :]
    high, low = split_ids(elem_nodes, node_rows, columns)
    obs_high, obs_low = split_ids(obs_nodes, node_rows, columns)
    basal_drag = jnp.exp(friction) * basal_area
    stack = pltpu.VMEM((4 * rows, columns), jnp.bfloat16)
    total = pltpu.VMEM((4 * rows, columns), jnp.float32)

    def spread(field):
        wide = ghosted(field)
        room = ((0, 0), (0, RIM - node_rows - 2))
        rim = jnp.concatenate([jnp.pad(wide[:, :, 0], room), jnp.pad(wide[:, :, -1], room)], axis=1)
        gap = jnp.zeros((2, rows - node_rows - 3, columns), jnp.float32)
        return jnp.concatenate([wide[:, :, 1:-1], rim[:, None, :], gap], axis=1)

    def finish(partial):
        both = lax.psum(partial, "sub")
        rim = both[:, node_rows + 2]
        left = rim[:, : node_rows + 2, None]
        right = rim[:, RIM : RIM + node_rows + 2, None]
        return reduce_rims(jnp.concatenate([left, both[:, : node_rows + 2], right], axis=2))

    coefficient = call(
        viscosity_kernel, (1, elements), [stack], spread(state_vel), high, low, elem_geom, scale
    )

    def operate(field):
        partial = call(
            operate_kernel,
            (2, rows, columns),
            [stack, total],
            spread(field),
            high,
            low,
            elem_geom,
            coefficient,
        )
        return finish(partial) + basal_drag * field

    def solve_field(right_side):
        solution = jnp.zeros_like(right_side)
        residual = right_side
        direction = right_side
        norm_now = norm_sum(residual)
        for iteration in range(CG_ITERS):
            applied = operate(direction)
            step_size = norm_now / lax.psum(jnp.sum(direction * applied), ("wide", "narrow"))
            solution = solution + step_size * direction
            residual = residual - step_size * applied
            if iteration + 1 < CG_ITERS:
                norm_next = norm_sum(residual)
                direction = residual + norm_next / norm_now * direction
                norm_now = norm_next
        return solution

    owners = lax.axis_size(("wide", "narrow"))
    capacity = obs_angle.shape[0] // owners
    tangent_vel = solve_field(-basal_drag * direction_beta * state_vel)
    weight_x = obs_bary * jnp.cos(obs_angle)
    weight_y = obs_bary * jnp.sin(obs_angle)
    readings = call(
        read_kernel,
        (1, obs_angle.shape[0]),
        [stack],
        spread(tangent_vel),
        obs_high,
        obs_low,
        weight_x,
        weight_y,
    ).reshape(owners, capacity)
    returned = lax.all_to_all(readings, ("wide", "narrow"), split_axis=0, concat_axis=0, tiled=True)
    target = pix_dest[:, 0]
    onehot = (target[:, None] == jnp.arange(owners, dtype=jnp.int32)[None, :]).astype(jnp.int32)
    running = jnp.cumsum(onehot, axis=0, dtype=jnp.int32)
    slot_rank = jnp.sum(jnp.where(onehot == 1, running, 0), axis=1) - 1
    slot_index = target * capacity + slot_rank
    weighted = weigh_rows(returned.reshape(-1)[slot_index], pix_prec, pix_couple)
    outgoing = (
        jnp.zeros((owners * capacity,), jnp.float32)
        .at[slot_index]
        .set(weighted)
        .reshape(owners, capacity)
    )
    arrived = lax.all_to_all(outgoing, ("wide", "narrow"), split_axis=0, concat_axis=0, tiled=True)
    partial = call(
        spread_kernel,
        (2, rows, columns),
        [total],
        arrived.reshape(1, -1),
        obs_high,
        obs_low,
        weight_x,
        weight_y,
    )
    adjoint = solve_field(finish(partial))
    hess_vec = -basal_drag * (state_vel[0] * adjoint[0] + state_vel[1] * adjoint[1])
    return (tangent_vel, hess_vec)


def solution(mesh):
    placed = (
        P(None, ("groups", "wide"), "narrow"),
        P(("groups", "wide"), "narrow"),
        P(("groups", "wide"), "narrow"),
        P(("groups", "wide"), "narrow"),
        P(None, ("groups", "wide", "narrow", "sub")),
        P(None, ("groups", "wide", "narrow", "sub")),
        P(("groups", "wide", "narrow", "sub")),
        P(("groups", "wide", "narrow")),
        P(("groups", "wide", "narrow", "sub"), None),
        P(("groups", "wide", "narrow", "sub")),
        P(("groups", "wide", "narrow", "sub")),
        P(None, ("groups", "wide", "narrow", "sub")),
        P(None, ("groups", "wide", "narrow", "sub")),
        P(("groups", "wide", "narrow", "sub")),
    )
    return jax.shard_map(
        per_device,
        mesh=mesh,
        in_specs=placed,
        out_specs=(P(None, ("groups", "wide"), "narrow"), P(("groups", "wide"), "narrow")),
        check_vma=False,
    )
```

```python
import functools

import jax
import jax.numpy as jnp
from jax import lax
from jax.experimental import pallas as pl
from jax.experimental.pallas import tpu as pltpu
from jax.sharding import PartitionSpec as P

CG_ITERS = 2

GLEN_B = 1.0
STRAIN_FLOOR = 0.01
RIM = 128
CHUNK = 512


def padded(block, sides, width):
    for axis, dim in sides:
        count = lax.axis_size(axis)
        forward = [(i, i + 1) for i in range(count - 1)]
        backward = [(target, source) for source, target in forward]
        low = lax.ppermute(
            lax.slice_in_dim(block, block.shape[dim] - width, None, axis=dim), axis, forward
        )
        high = lax.ppermute(lax.slice_in_dim(block, 0, width, axis=dim), axis, backward)
        block = jnp.concatenate([low, block, high], axis=dim)
    return block


def split_pair(values):
    high = values.astype(jnp.bfloat16)
    low = (values - high.astype(jnp.float32)).astype(jnp.bfloat16)
    return high, low


def stack_field(field):
    high_x, low_x = split_pair(field[0])
    high_y, low_y = split_pair(field[1])
    return jnp.concatenate([high_x, high_y, low_x, low_y], axis=0)


def column_onehot(low_ids, width):
    place = lax.broadcasted_iota(jnp.int32, (width, low_ids.shape[1]), 0)
    return jnp.where(place == low_ids, 1.0, 0.0).astype(jnp.bfloat16)


def row_mask(high_ids, rows):
    return lax.broadcasted_iota(jnp.int32, (rows, high_ids.shape[1]), 0) == high_ids


def pick(stacked, mask, onehot):
    rows = mask.shape[0]
    grown = jnp.dot(stacked, onehot, preferred_element_type=jnp.float32)
    both = grown[: 2 * rows] + grown[2 * rows :]
    value_x = jnp.sum(jnp.where(mask, both[:rows], 0.0), axis=0, keepdims=True)
    value_y = jnp.sum(jnp.where(mask, both[rows:], 0.0), axis=0, keepdims=True)
    return value_x, value_y


def masked_stack(mask, value_x, value_y):
    parts = split_f32(value_x, value_y)
    return jnp.concatenate(
        [jnp.where(mask, part, 0.0).astype(jnp.bfloat16) for part in parts], axis=0
    )


def split_f32(value_x, value_y):
    high_x = value_x.astype(jnp.bfloat16).astype(jnp.float32)
    high_y = value_y.astype(jnp.bfloat16).astype(jnp.float32)
    return high_x, high_y, value_x - high_x, value_y - high_y


def add_in(stacks, onehots):
    left = jnp.concatenate(stacks, axis=1)
    right = jnp.concatenate(onehots, axis=1)
    return lax.dot_general(
        left, right, (((1,), (1,)), ((), ())), preferred_element_type=jnp.float32
    )


def unstack(total):
    both = total[: total.shape[0] // 2] + total[total.shape[0] // 2 :]
    rows = both.shape[0] // 2
    return both[:rows], both[rows:]


def strain_rows(values, grad):
    value_x, value_y = values
    strain_xx = grad[0] * value_x[0] + grad[1] * value_x[1] + grad[2] * value_x[2]
    strain_yy = grad[3] * value_y[0] + grad[4] * value_y[1] + grad[5] * value_y[2]
    strain_xy = 0.5 * (
        (grad[3] * value_x[0] + grad[0] * value_y[0])
        + (grad[4] * value_x[1] + grad[1] * value_y[1])
        + (grad[5] * value_x[2] + grad[2] * value_y[2])
    )
    return strain_xx, strain_yy, strain_xy


def chunk_of(step):
    return pl.ds(pl.multiple_of(step * CHUNK, CHUNK), CHUNK)


def gather_chunk(stacked, high_ref, low_ref, cols, rows, width):
    masks, onehots, value_x, value_y = [], [], [], []
    for a in range(3):
        mask = row_mask(high_ref[a : a + 1, cols], rows)
        onehot = column_onehot(low_ref[a : a + 1, cols], width)
        got_x, got_y = pick(stacked, mask, onehot)
        masks.append(mask)
        onehots.append(onehot)
        value_x.append(got_x)
        value_y.append(got_y)
    return masks, onehots, (value_x, value_y)


def viscosity_loop(stack_ref, high_ref, low_ref, geom_ref, scale_ref, coef_ref, rows):
    width = stack_ref.shape[1]

    def body(step, carry):
        cols = chunk_of(step)
        _, _, values = gather_chunk(stack_ref[...], high_ref, low_ref, cols, rows, width)
        grad = [geom_ref[i : i + 1, cols] for i in range(6)]
        exx, eyy, exy = strain_rows(values, grad)
        effective = exx * exx + eyy * eyy + exx * eyy + exy * exy + STRAIN_FLOOR
        viscosity = 0.5 * GLEN_B * jnp.exp(jnp.log(effective) * (-1.0 / 3.0))
        coef_ref[:, cols] = 2.0 * viscosity * scale_ref[:, cols]
        return carry

    lax.fori_loop(0, high_ref.shape[1] // CHUNK, body, 0)


def operate_loop(stack_ref, high_ref, low_ref, geom_ref, coef_ref, total_ref, rows):
    width = stack_ref.shape[1]
    total_ref[...] = jnp.zeros_like(total_ref)

    def body(step, carry):
        cols = chunk_of(step)
        masks, onehots, values = gather_chunk(
            stack_ref[...], high_ref, low_ref, cols, rows, width
        )
        grad = [geom_ref[i : i + 1, cols] for i in range(6)]
        coefficient = coef_ref[:, cols]
        exx, eyy, exy = strain_rows(values, grad)
        sxx = coefficient * (2.0 * exx + eyy)
        syy = coefficient * (exx + 2.0 * eyy)
        sxy = coefficient * exy
        stacks = [
            masked_stack(
                masks[a],
                sxx * grad[a] + sxy * grad[3 + a],
                syy * grad[3 + a] + sxy * grad[a],
            )
            for a in range(3)
        ]
        total_ref[...] += add_in(stacks, onehots)
        return carry

    lax.fori_loop(0, high_ref.shape[1] // CHUNK, body, 0)


def read_loop(stack_ref, high_ref, low_ref, weight_x_ref, weight_y_ref, read_ref, rows):
    width = stack_ref.shape[1]

    def body(step, carry):
        cols = chunk_of(step)
        _, _, values = gather_chunk(stack_ref[...], high_ref, low_ref, cols, rows, width)
        total = 0.0
        for a in range(3):
            total = total + (
                weight_x_ref[a : a + 1, cols] * values[0][a]
                + weight_y_ref[a : a + 1, cols] * values[1][a]
            )
        read_ref[:, cols] = total
        return carry

    lax.fori_loop(0, high_ref.shape[1] // CHUNK, body, 0)


def spread_loop(arrived_ref, high_ref, low_ref, weight_x_ref, weight_y_ref, total_ref, rows):
    width = total_ref.shape[1]
    total_ref[...] = jnp.zeros_like(total_ref)

    def body(step, carry):
        cols = chunk_of(step)
        arrived = arrived_ref[:, cols]
        stacks, onehots = [], []
        for a in range(3):
            mask = row_mask(high_ref[a : a + 1, cols], rows)
            onehots.append(column_onehot(low_ref[a : a + 1, cols], width))
            stacks.append(
                masked_stack(
                    mask,
                    arrived * weight_x_ref[a : a + 1, cols],
                    arrived * weight_y_ref[a : a + 1, cols],
                )
            )
        total_ref[...] += add_in(stacks, onehots)
        return carry

    lax.fori_loop(0, high_ref.shape[1] // CHUNK, body, 0)


def viscosity_kernel(field_ref, high_ref, low_ref, geom_ref, scale_ref, coef_ref, stack_ref):
    stack_ref[...] = stack_field(field_ref)
    viscosity_loop(
        stack_ref, high_ref, low_ref, geom_ref, scale_ref, coef_ref, field_ref.shape[1]
    )


def operate_kernel(
    field_ref, high_ref, low_ref, geom_ref, coef_ref, out_ref, stack_ref, total_ref
):
    stack_ref[...] = stack_field(field_ref)
    operate_loop(
        stack_ref, high_ref, low_ref, geom_ref, coef_ref, total_ref, field_ref.shape[1]
    )
    out_ref[0], out_ref[1] = unstack(total_ref[...])


def read_kernel(field_ref, high_ref, low_ref, wx_ref, wy_ref, read_ref, stack_ref):
    stack_ref[...] = stack_field(field_ref)
    read_loop(stack_ref, high_ref, low_ref, wx_ref, wy_ref, read_ref, field_ref.shape[1])


def spread_kernel(arrived_ref, high_ref, low_ref, wx_ref, wy_ref, out_ref, total_ref):
    spread_loop(arrived_ref, high_ref, low_ref, wx_ref, wy_ref, total_ref, out_ref.shape[1])
    out_ref[0], out_ref[1] = unstack(total_ref[...])


def call(kernel, out, scratch, *args):
    return pl.pallas_call(
        kernel,
        out_shape=jax.ShapeDtypeStruct(out, jnp.float32),
        in_specs=[pl.BlockSpec(memory_space=pltpu.VMEM)] * len(args),
        out_specs=pl.BlockSpec(memory_space=pltpu.VMEM),
        scratch_shapes=scratch,
        compiler_params=pltpu.CompilerParams(vmem_limit_bytes=48 * 1024 * 1024),
    )(*args)


def split_ids(ids, node_rows, columns):
    row = ids // (columns + 2)
    col = ids % (columns + 2)
    left, right = col == 0, col == columns + 1
    high = jnp.where(left | right, node_rows + 2, row)
    low = jnp.where(left, row, jnp.where(right, row + RIM, col - 1))
    return high, low


def weigh_rows(readings, precision, couple):
    grid_read = readings.reshape(-1, 128)
    grid_prec = precision.reshape(-1, 128)
    grid_couple = couple.reshape(-1, 128)
    column = jnp.arange(128)[None, :]
    next_prec = jnp.concatenate([grid_prec[:, 1:], grid_prec[:, :1]], axis=1)
    link_weight = jnp.where(column < 127, grid_couple * jnp.sqrt(grid_prec * next_prec), 0.0)
    zero_col = jnp.zeros_like(grid_read[:, :1])
    next_read = jnp.concatenate([grid_read[:, 1:], zero_col], axis=1)
    prev_read = jnp.concatenate([zero_col, grid_read[:, :-1]], axis=1)
    prev_link = jnp.concatenate([zero_col, link_weight[:, :-1]], axis=1)
    return (grid_prec * grid_read - link_weight * next_read - prev_link * prev_read).reshape(-1)


def ghosted(field):
    return padded(field, (("wide", 1), ("narrow", 2)), 1)


def reduce_rims(summed):
    side_cols = jnp.concatenate([summed[:, :, :1], summed[:, :, -1:]], axis=2)
    beside = padded(side_cols, (("narrow", 2),), 1)
    middle = summed[:, :, 1:-1]
    middle = middle.at[:, :, 0].add(beside[:, :, 0]).at[:, :, -1].add(beside[:, :, 3])
    side_rows = jnp.concatenate([middle[:, :1], middle[:, -1:]], axis=1)
    across = padded(side_rows, (("wide", 1),), 1)
    interior = middle[:, 1:-1]
    return interior.at[:, 0].add(across[:, 0]).at[:, -1].add(across[:, 3])


def norm_sum(residual):
    return lax.psum(jnp.sum(residual * residual), ("wide", "narrow"))


def per_device(
    state_vel,
    friction,
    basal_area,
    direction_beta,
    elem_nodes,
    elem_geom,
    elem_thick,
    live_blocks,
    pix_dest,
    pix_prec,
    pix_couple,
    obs_nodes,
    obs_bary,
    obs_angle,
):
    node_rows, columns = friction.shape
    rows = -(-(node_rows + 3) // 8) * 8
    elements = elem_nodes.shape[1]
    core_index = lax.axis_index("sub")
    alive = jnp.arange(elements, dtype=jnp.int32) // 128 < live_blocks[core_index]
    scale = jnp.where(alive, elem_thick * elem_geom[6], 0.0)[None, :]
    high, low = split_ids(elem_nodes, node_rows, columns)
    obs_high, obs_low = split_ids(obs_nodes, node_rows, columns)
    basal_drag = jnp.exp(friction) * basal_area
    stack = pltpu.VMEM((4 * rows, columns), jnp.bfloat16)
    total = pltpu.VMEM((4 * rows, columns), jnp.float32)

    def spread(field):
        wide = ghosted(field)
        room = ((0, 0), (0, RIM - node_rows - 2))
        rim = jnp.concatenate([jnp.pad(wide[:, :, 0], room), jnp.pad(wide[:, :, -1], room)], axis=1)
        gap = jnp.zeros((2, rows - node_rows - 3, columns), jnp.float32)
        return jnp.concatenate([wide[:, :, 1:-1], rim[:, None, :], gap], axis=1)

    def finish(partial):
        both = lax.psum(partial, "sub")
        rim = both[:, node_rows + 2]
        left = rim[:, : node_rows + 2, None]
        right = rim[:, RIM : RIM + node_rows + 2, None]
        return reduce_rims(jnp.concatenate([left, both[:, : node_rows + 2], right], axis=2))

    coefficient = call(
        viscosity_kernel, (1, elements), [stack], spread(state_vel), high, low, elem_geom, scale
    )

    def operate(field):
        partial = call(
            operate_kernel,
            (2, rows, columns),
            [stack, total],
            spread(field),
            high,
            low,
            elem_geom,
            coefficient,
        )
        return finish(partial) + basal_drag * field

    def solve_field(right_side):
        solution = jnp.zeros_like(right_side)
        residual = right_side
        direction = right_side
        norm_now = norm_sum(residual)
        for iteration in range(CG_ITERS):
            applied = operate(direction)
            step_size = norm_now / lax.psum(jnp.sum(direction * applied), ("wide", "narrow"))
            solution = solution + step_size * direction
            residual = residual - step_size * applied
            if iteration + 1 < CG_ITERS:
                norm_next = norm_sum(residual)
                direction = residual + norm_next / norm_now * direction
                norm_now = norm_next
        return solution

    owners = lax.axis_size(("wide", "narrow"))
    capacity = obs_angle.shape[0] // owners
    tangent_vel = solve_field(-basal_drag * direction_beta * state_vel)
    weight_x = obs_bary * jnp.cos(obs_angle)
    weight_y = obs_bary * jnp.sin(obs_angle)
    readings = call(
        read_kernel,
        (1, obs_angle.shape[0]),
        [stack],
        spread(tangent_vel),
        obs_high,
        obs_low,
        weight_x,
        weight_y,
    ).reshape(owners, capacity)
    returned = lax.all_to_all(readings, ("wide", "narrow"), split_axis=0, concat_axis=0, tiled=True)
    target = pix_dest[:, 0]
    onehot = (target[:, None] == jnp.arange(owners, dtype=jnp.int32)[None, :]).astype(jnp.int32)
    running = jnp.cumsum(onehot, axis=0, dtype=jnp.int32)
    slot_rank = jnp.sum(jnp.where(onehot == 1, running, 0), axis=1) - 1
    slot_index = target * capacity + slot_rank
    weighted = weigh_rows(returned.reshape(-1)[slot_index], pix_prec, pix_couple)
    outgoing = (
        jnp.zeros((owners * capacity,), jnp.float32)
        .at[slot_index]
        .set(weighted)
        .reshape(owners, capacity)
    )
    arrived = lax.all_to_all(outgoing, ("wide", "narrow"), split_axis=0, concat_axis=0, tiled=True)
    partial = call(
        spread_kernel,
        (2, rows, columns),
        [total],
        arrived.reshape(1, -1),
        obs_high,
        obs_low,
        weight_x,
        weight_y,
    )
    adjoint = solve_field(finish(partial))
    hess_vec = -basal_drag * (state_vel[0] * adjoint[0] + state_vel[1] * adjoint[1])
    return (tangent_vel, hess_vec)


def node_ids(ids, node_rows, columns):
    row = ids // (columns + 2)
    col = ids % (columns + 2)
    left, right = col == 0, col == columns + 1
    inner = jnp.where(row == 0, node_rows, jnp.where(row == node_rows + 1, row, row - 1))
    high = jnp.where(left | right, node_rows + 2, inner)
    low = jnp.where(left, row, jnp.where(right, row + RIM, col - 1))
    return high, low


SIDES = [(dw, dn) for dw in (-1, 0, 1) for dn in (-1, 0, 1)]
TILE = 8


def whole_kernel(
    wide,
    narrow,
    state_ref,
    friction_ref,
    area_ref,
    beta_ref,
    high_ref,
    low_ref,
    geom_ref,
    scale_ref,
    dest_ref,
    prec_ref,
    couple_ref,
    obs_high_ref,
    obs_low_ref,
    wx_ref,
    wy_ref,
    tangent_ref,
    hess_ref,
    stack_ref,
    total_ref,
    coef_ref,
    drag_ref,
    vel_ref,
    p_ref,
    r_ref,
    x_ref,
    q_ref,
    field_send,
    field_recv,
    rim_send,
    rim_recv,
    sum_send,
    sum_recv,
    pix_send,
    pix_recv,
    field_ss,
    field_rs,
    rim_ss,
    rim_rs,
    sum_ss,
    sum_rs,
    pix_ss,
    pix_rs,
):
    node_rows, columns = friction_ref.shape
    rows = vel_ref.shape[1]
    count = wide * narrow
    my_w = lax.axis_index("wide")
    my_n = lax.axis_index("narrow")
    my_s = lax.axis_index("sub")
    me = my_w * narrow + my_n
    f32 = jnp.float32

    def place_of(q):
        return {"wide": q // narrow, "narrow": lax.rem(q, narrow), "sub": my_s}

    partner = {"wide": my_w, "narrow": my_n, "sub": 1 - my_s}
    barrier = pltpu.get_barrier_semaphore()
    pl.semaphore_signal(barrier, inc=1, device_id=partner, device_id_type=pl.DeviceIdType.MESH)
    for k in range(1, count):
        pl.semaphore_signal(
            barrier,
            inc=1,
            device_id=place_of(lax.rem(me + k, count)),
            device_id_type=pl.DeviceIdType.MESH,
        )
    pl.semaphore_wait(barrier, count)

    row_at = lax.broadcasted_iota(jnp.int32, (rows, columns), 0)
    lane_at = lax.broadcasted_iota(jnp.int32, (rows, columns), 1)
    eye_row = lax.broadcasted_iota(jnp.int32, (rows, RIM), 0)
    eye_lane = lax.broadcasted_iota(jnp.int32, (rows, RIM), 1)
    eye_row = jnp.where(
        eye_row < node_rows,
        eye_row + 1,
        jnp.where(eye_row == node_rows, 0, jnp.where(eye_row == node_rows + 1, eye_row, -1)),
    )
    eye = eye_row == eye_lane
    rim_lane = lax.broadcasted_iota(jnp.int32, (1, RIM), 1)

    def exists(dw, dn):
        w, n = my_w + dw, my_n + dn
        return (w >= 0) & (w < wide) & (n >= 0) & (n < narrow)

    has_up, has_down = my_w > 0, my_w < wide - 1
    has_left, has_right = my_n > 0, my_n < narrow - 1
    rim_row = jnp.where(lane_at >= RIM, lane_at - RIM, lane_at)
    rim_side = ((lane_at < RIM) & has_left) | ((lane_at >= RIM) & has_right)
    rim_in = (
        ((rim_row >= 1) & (rim_row <= node_rows))
        | ((rim_row == 0) & has_up)
        | ((rim_row == node_rows + 1) & has_down)
    )
    inside = (
        (row_at < node_rows)
        | ((row_at == node_rows) & has_up)
        | ((row_at == node_rows + 1) & has_down)
        | ((row_at == node_rows + 2) & rim_side & rim_in)
    )

    def col_lanes(field, lane):
        column = field[:, lane : lane + 1]
        return jnp.sum(jnp.where(eye, column, 0.0), axis=0, keepdims=True)

    def lanes_col(lanes):
        return jnp.sum(jnp.where(eye, lanes, 0.0), axis=1, keepdims=True)

    def rim_copy(k, slot):
        dw, dn = SIDES[slot]
        return pltpu.make_async_remote_copy(
            src_ref=rim_send.at[k],
            dst_ref=rim_recv.at[k, 8 - slot],
            send_sem=rim_ss.at[k, slot],
            recv_sem=rim_rs.at[k, 8 - slot],
            device_id={"wide": my_w + dw, "narrow": my_n + dn, "sub": my_s},
            device_id_type=pl.DeviceIdType.MESH,
        )

    def rim_landed(k, slot):
        dw, dn = SIDES[slot]
        return pltpu.make_async_remote_copy(
            src_ref=rim_send.at[k],
            dst_ref=rim_recv.at[k, slot],
            send_sem=rim_ss.at[k, slot],
            recv_sem=rim_rs.at[k, slot],
            device_id={"wide": my_w + dw, "narrow": my_n + dn, "sub": my_s},
            device_id_type=pl.DeviceIdType.MESH,
        )

    def rim_start(k, fields):
        lines = []
        for at in (node_rows, 0, node_rows - 1, node_rows + 1, node_rows + 2):
            lines += [field[at : at + 1] for field in fields]
        lines += [
            jnp.concatenate([col_lanes(field, 0), col_lanes(field, columns - 1)], axis=1)
            for field in fields
        ]
        for i, line in enumerate(lines):
            rim_send[k, i : i + 1, :] = line
        for slot, side in enumerate(SIDES):
            if side != (0, 0):

                @pl.when(exists(*side))
                def _():
                    rim_copy(k, slot).start()

    def moved(lanes, dw):
        if dw == 0:
            return lanes
        if dw < 0:
            turned = pltpu.roll(lanes, (RIM - node_rows) % RIM, 1)
            return jnp.where(rim_lane < 2, turned, 0.0)
        turned = pltpu.roll(lanes, node_rows, 1)
        keep = (rim_lane == node_rows) | (rim_lane == node_rows + 1)
        return jnp.where(keep, turned, 0.0)

    def rim_finish(k, fields):
        for slot, side in enumerate(SIDES):
            if side != (0, 0):

                @pl.when(exists(*side))
                def _():
                    rim_landed(k, slot).wait_recv()
                    rim_landed(k, slot).wait_send()

        done = []
        for c, field in enumerate(fields):

            def got(dw, dn, line, low, size):
                slot = SIDES.index((dw, dn))
                at = 2 * line + c
                value = rim_recv[k, slot, at : at + 1, low : low + size]
                return jnp.where(exists(dw, dn), value, 0.0)

            left_rim = jnp.zeros((1, RIM), f32)
            right_rim = jnp.zeros((1, RIM), f32)
            left_col = jnp.zeros((1, RIM), f32)
            right_col = jnp.zeros((1, RIM), f32)
            for dw in (-1, 1):
                left_rim = left_rim + moved(got(dw, 0, 4, 0, RIM), dw)
                right_rim = right_rim + moved(got(dw, 0, 4, RIM, RIM), dw)
            for dw in (0, -1, 1):
                left_col = left_col + moved(got(dw, -1, 4, RIM, RIM), dw)
                left_rim = left_rim + moved(got(dw, -1, 5, RIM, RIM), dw)
                right_col = right_col + moved(got(dw, 1, 4, 0, RIM), dw)
                right_rim = right_rim + moved(got(dw, 1, 5, 0, RIM), dw)
            result = field
            for at, dw, line in (
                (node_rows, -1, 2),
                (0, -1, 3),
                (node_rows - 1, 1, 0),
                (node_rows + 1, 1, 1),
            ):
                result = result + jnp.where(row_at == at, got(dw, 0, line, 0, columns), 0.0)
            rim = jnp.concatenate([left_rim, right_rim], axis=1)
            result = result + jnp.where(row_at == node_rows + 2, rim, 0.0)
            result = result + jnp.where(lane_at == 0, lanes_col(left_col), 0.0)
            result = result + jnp.where(lane_at == columns - 1, lanes_col(right_col), 0.0)
            done.append(jnp.where(inside, result, 0.0))
        return done

    def all_copy(send, recv, ss, rs, k, target, slot):
        return pltpu.make_async_remote_copy(
            src_ref=send,
            dst_ref=recv.at[k, slot],
            send_sem=ss.at[k, target],
            recv_sem=rs.at[k, slot],
            device_id=place_of(target),
            device_id_type=pl.DeviceIdType.MESH,
        )

    def sum_start(k, *values):
        for i, value in enumerate(values):
            sum_send[k, i : i + 1, :] = jnp.broadcast_to(value, (1, 128))
        for j in range(1, count):
            q = lax.rem(me + j, count)
            all_copy(sum_send.at[k], sum_recv, sum_ss, sum_rs, k, q, me).start()
        sum_recv[k, me] = sum_send[k]

    def sum_finish(k):
        for j in range(1, count):
            q = lax.rem(me + j, count)
            copy = all_copy(sum_send.at[k], sum_recv, sum_ss, sum_rs, k, q, q)
            copy.wait_recv()
            copy.wait_send()
        total = sum_recv[k, 0]
        for q in range(1, count):
            total = total + sum_recv[k, q]
        return total[0:1, 0:1], total[1:2, 0:1]

    def pix_trade(k):
        for j in range(1, count):
            q = lax.rem(me + j, count)
            all_copy(pix_send.at[k, q], pix_recv, pix_ss, pix_rs, k, q, me).start()
        pix_recv[k, me] = pix_send[k, me]
        for j in range(1, count):
            q = lax.rem(me + j, count)
            copy = all_copy(pix_send.at[k, q], pix_recv, pix_ss, pix_rs, k, q, q)
            copy.wait_recv()
            copy.wait_send()

    def core_sum(k):
        field_send[k, 0], field_send[k, 1] = unstack(total_ref[...])
        copy = pltpu.make_async_remote_copy(
            src_ref=field_send.at[k],
            dst_ref=field_recv.at[k],
            send_sem=field_ss.at[k],
            recv_sem=field_rs.at[k],
            device_id=partner,
            device_id_type=pl.DeviceIdType.MESH,
        )
        copy.start()
        copy.wait()
        return [field_send[k, c] + field_recv[k, c] for c in range(2)]

    def dot(a, b):
        down = jnp.sum(a * b, axis=0, keepdims=True)
        return jnp.sum(down, axis=1, keepdims=True)

    def both(a_ref, b_ref, size):
        return dot(a_ref[0, :size], b_ref[0, :size]) + dot(a_ref[1, :size], b_ref[1, :size])

    def solve(field_at, rim_at, sum_at):
        for c in range(2):
            p_ref[c] = r_ref[c]
        norm_now = None
        for step in range(CG_ITERS):
            stack_ref[...] = stack_field(p_ref)
            operate_loop(stack_ref, high_ref, low_ref, geom_ref, coef_ref, total_ref, rows)
            local = core_sum(field_at + step)
            rim_start(rim_at + step, local)
            energy = dot(local[0], p_ref[0]) + dot(local[1], p_ref[1])
            for c in range(2):
                field = p_ref[c, :node_rows]
                energy = energy + dot(drag_ref[:node_rows] * field, field)
            norm = both(r_ref, r_ref, node_rows)
            sum_start(sum_at + 2 * step, norm, energy)
            applied = rim_finish(rim_at + step, local)
            for c in range(2):
                q_ref[c] = applied[c] + drag_ref[...] * p_ref[c]
            norm_now, energy = sum_finish(sum_at + 2 * step)
            alpha = norm_now / energy
            for c in range(2):
                if step == 0:
                    x_ref[c] = alpha * p_ref[c]
                else:
                    x_ref[c] = x_ref[c] + alpha * p_ref[c]
            if step + 1 < CG_ITERS:
                for c in range(2):
                    r_ref[c] = r_ref[c] - alpha * q_ref[c]
                norm = both(r_ref, r_ref, node_rows)
                sum_start(sum_at + 2 * step + 1, norm)
                norm_next, _ = sum_finish(sum_at + 2 * step + 1)
                ratio = norm_next / norm_now
                for c in range(2):
                    p_ref[c] = r_ref[c] + ratio * p_ref[c]

    sum_send[...] = jnp.zeros_like(sum_send)
    rim_send[...] = jnp.zeros_like(rim_send)
    pix_send[...] = jnp.zeros_like(pix_send)
    gap = jnp.zeros((rows - node_rows, columns), f32)

    def grown(value):
        return jnp.concatenate([value, gap], axis=0)

    vel = [grown(state_ref[0]), grown(state_ref[1])]
    rim_start(0, vel)
    other = [grown(jnp.exp(friction_ref[...]) * area_ref[...]), grown(beta_ref[...])]
    rim_start(1, other)
    vel_ref[0], vel_ref[1] = rim_finish(0, vel)
    drag, beta = rim_finish(1, other)
    drag_ref[...] = drag
    for c in range(2):
        r_ref[c] = -drag * beta * vel_ref[c]
    stack_ref[...] = stack_field(vel_ref)
    viscosity_loop(stack_ref, high_ref, low_ref, geom_ref, scale_ref, coef_ref, rows)
    solve(0, 2, 0)
    tangent_ref[...] = x_ref[:, :node_rows]

    capacity = obs_high_ref.shape[1] // count
    lines = capacity // 128
    stack_ref[...] = stack_field(x_ref)

    def read(step, carry):
        cols = pl.ds(pl.multiple_of(step * capacity, 128), capacity)
        _, _, values = gather_chunk(
            stack_ref[...], obs_high_ref, obs_low_ref, cols, rows, columns
        )
        total = jnp.zeros((1, capacity), f32)
        for a in range(3):
            total = total + (
                wx_ref[a : a + 1, cols] * values[0][a] + wy_ref[a : a + 1, cols] * values[1][a]
            )
        for j in range(lines):
            pix_send[0, step, j : j + 1, :] = total[:, j * 128 : (j + 1) * 128]
        return carry

    lax.fori_loop(0, count, read, 0)
    pix_trade(0)

    dest = dest_ref[...]
    pixel_rows = dest.shape[0]
    named = jnp.concatenate(
        [jnp.where(dest == q, 1.0, 0.0) for q in range(count)], axis=0
    ).astype(jnp.bfloat16)
    first = lax.broadcasted_iota(jnp.int32, (128, 128), 0)
    second = lax.broadcasted_iota(jnp.int32, (128, 128), 1)
    before = jnp.where(first < second, 1.0, 0.0).astype(jnp.bfloat16)
    ones = jnp.ones((128, 128), jnp.bfloat16)
    within = jnp.dot(named, before, preferred_element_type=f32)
    per_row = jnp.dot(named, ones, preferred_element_type=f32).astype(jnp.bfloat16)
    size = count * pixel_rows
    first = lax.broadcasted_iota(jnp.int32, (size, size), 0)
    second = lax.broadcasted_iota(jnp.int32, (size, size), 1)
    start = first // pixel_rows * pixel_rows
    above = jnp.where((second >= start) & (second < first), 1.0, 0.0).astype(jnp.bfloat16)
    ranks = within + jnp.dot(above, per_row, preferred_element_type=f32)
    rank = jnp.zeros((pixel_rows, 128), f32)
    for q in range(count):
        rank = rank + jnp.where(dest == q, ranks[q * pixel_rows : (q + 1) * pixel_rows], 0.0)
    rank = rank.astype(jnp.int32)
    slot_line = dest * TILE + rank // 128
    slot_lane = lax.rem(rank, 128)

    def flat(value):
        return jnp.concatenate([value[i : i + 1] for i in range(pixel_rows)], axis=1)

    table = count * TILE
    line_mask = row_mask(flat(slot_line), table)
    lane_hot = column_onehot(flat(slot_lane), 128)
    high, low = split_pair(pix_recv[0].reshape(table, 128))
    spread_out = jnp.dot(
        jnp.concatenate([high, low], axis=0), lane_hot, preferred_element_type=f32
    )
    spread_out = spread_out[:table] + spread_out[table:]
    line = jnp.sum(jnp.where(line_mask, spread_out, 0.0), axis=0, keepdims=True)
    reading = jnp.concatenate(
        [line[:, i * 128 : (i + 1) * 128] for i in range(pixel_rows)], axis=0
    )
    precision = prec_ref[...]
    column = lax.broadcasted_iota(jnp.int32, (pixel_rows, 128), 1)
    link = jnp.where(
        column < 127,
        couple_ref[...] * jnp.sqrt(precision * pltpu.roll(precision, 127, 1)),
        0.0,
    )
    weighted = (
        precision * reading
        - link * pltpu.roll(reading, 127, 1)
        - pltpu.roll(link, 1, 1) * pltpu.roll(reading, 1, 1)
    )
    weighted = flat(weighted)
    top = weighted.astype(jnp.bfloat16).astype(f32)
    left = jnp.concatenate(
        [jnp.where(line_mask, part, 0.0).astype(jnp.bfloat16) for part in (top, weighted - top)],
        axis=0,
    )
    out = lax.dot_general(
        left, lane_hot, (((1,), (1,)), ((), ())), preferred_element_type=f32
    )
    pix_send[1] = (out[:table] + out[table:]).reshape(count, TILE, 128)
    pix_trade(1)

    total_ref[...] = jnp.zeros_like(total_ref)

    def scatter(step, carry):
        cols = pl.ds(pl.multiple_of(step * capacity, 128), capacity)
        tile = pix_recv[1, step]
        arrived = jnp.concatenate([tile[j : j + 1] for j in range(lines)], axis=1)
        stacks, onehots = [], []
        for a in range(3):
            mask = row_mask(obs_high_ref[a : a + 1, cols], rows)
            onehots.append(column_onehot(obs_low_ref[a : a + 1, cols], columns))
            stacks.append(
                masked_stack(
                    mask, arrived * wx_ref[a : a + 1, cols], arrived * wy_ref[a : a + 1, cols]
                )
            )
        total_ref[...] += add_in(stacks, onehots)
        return carry

    lax.fori_loop(0, count, scatter, 0)
    local = core_sum(2)
    rim_start(4, local)
    r_ref[0], r_ref[1] = rim_finish(4, local)
    solve(3, 5, 3)
    hess_ref[...] = -drag_ref[:node_rows] * (
        state_ref[0] * x_ref[0, :node_rows] + state_ref[1] * x_ref[1, :node_rows]
    )


def fused_device(
    state_vel,
    friction,
    basal_area,
    direction_beta,
    elem_nodes,
    elem_geom,
    elem_thick,
    live_blocks,
    pix_dest,
    pix_prec,
    pix_couple,
    obs_nodes,
    obs_bary,
    obs_angle,
):
    node_rows, columns = friction.shape
    rows = -(-(node_rows + 3) // 8) * 8
    elements = elem_nodes.shape[1]
    wide, narrow = lax.axis_size("wide"), lax.axis_size("narrow")
    count = wide * narrow
    alive = jnp.arange(elements, dtype=jnp.int32) // 128 < live_blocks[lax.axis_index("sub")]
    scale = jnp.where(alive, elem_thick * elem_geom[6], 0.0)[None, :]
    high, low = node_ids(elem_nodes, node_rows, columns)
    obs_high, obs_low = node_ids(obs_nodes, node_rows, columns)
    weight_x = obs_bary * jnp.cos(obs_angle)
    weight_y = obs_bary * jnp.sin(obs_angle)
    f32 = jnp.float32
    pair = pltpu.VMEM((2, rows, columns), f32)
    args = (
        state_vel,
        friction,
        basal_area,
        direction_beta,
        high,
        low,
        elem_geom,
        scale,
        pix_dest.reshape(-1, 128),
        pix_prec.reshape(-1, 128),
        pix_couple.reshape(-1, 128),
        obs_high,
        obs_low,
        weight_x,
        weight_y,
    )
    dma = pltpu.SemaphoreType.DMA
    return pl.pallas_call(
        functools.partial(whole_kernel, wide, narrow),
        out_shape=(
            jax.ShapeDtypeStruct((2, node_rows, columns), f32),
            jax.ShapeDtypeStruct((node_rows, columns), f32),
        ),
        in_specs=[pl.BlockSpec(memory_space=pltpu.VMEM)] * len(args),
        out_specs=(pl.BlockSpec(memory_space=pltpu.VMEM),) * 2,
        scratch_shapes=[
            pltpu.VMEM((4 * rows, columns), jnp.bfloat16),
            pltpu.VMEM((4 * rows, columns), f32),
            pltpu.VMEM((1, elements), f32),
            pltpu.VMEM((rows, columns), f32),
            pair,
            pair,
            pair,
            pair,
            pair,
            pltpu.VMEM((5, 2, rows, columns), f32),
            pltpu.VMEM((5, 2, rows, columns), f32),
            pltpu.VMEM((7, 16, columns), f32),
            pltpu.VMEM((7, 9, 16, columns), f32),
            pltpu.VMEM((6, 8, 128), f32),
            pltpu.VMEM((6, count, 8, 128), f32),
            pltpu.VMEM((2, count, TILE, 128), f32),
            pltpu.VMEM((2, count, TILE, 128), f32),
            dma((5,)),
            dma((5,)),
            dma((7, 9)),
            dma((7, 9)),
            dma((6, count)),
            dma((6, count)),
            dma((2, count)),
            dma((2, count)),
        ],
        compiler_params=pltpu.CompilerParams(
            collective_id=0, has_side_effects=True, vmem_limit_bytes=48 * 1024 * 1024
        ),
    )(*args)


def choose(*args):
    count = lax.axis_size("wide") * lax.axis_size("narrow")
    capacity = args[-1].shape[0] // count
    columns = args[1].shape[1]
    if capacity % 128 == 0 and capacity <= 128 * TILE and columns == 2 * RIM and args[1].shape[0] + 2 <= RIM:
        return fused_device(*args)
    return per_device(*args)


def solution(mesh):
    placed = (
        P(None, ("groups", "wide"), "narrow"),
        P(("groups", "wide"), "narrow"),
        P(("groups", "wide"), "narrow"),
        P(("groups", "wide"), "narrow"),
        P(None, ("groups", "wide", "narrow", "sub")),
        P(None, ("groups", "wide", "narrow", "sub")),
        P(("groups", "wide", "narrow", "sub")),
        P(("groups", "wide", "narrow")),
        P(("groups", "wide", "narrow", "sub"), None),
        P(("groups", "wide", "narrow", "sub")),
        P(("groups", "wide", "narrow", "sub")),
        P(None, ("groups", "wide", "narrow", "sub")),
        P(None, ("groups", "wide", "narrow", "sub")),
        P(("groups", "wide", "narrow", "sub")),
    )
    return jax.shard_map(
        choose,
        mesh=mesh,
        in_specs=placed,
        out_specs=(P(None, ("groups", "wide"), "narrow"), P(("groups", "wide"), "narrow")),
        check_vma=False,
    )
```

```python
import functools

import jax
import jax.numpy as jnp
from jax import lax
from jax.experimental import pallas as pl
from jax.experimental.pallas import tpu as pltpu
from jax.sharding import PartitionSpec as P

CG_ITERS = 2

GLEN_B = 1.0
STRAIN_FLOOR = 0.01
RIM = 128
CHUNK = 512


def padded(block, sides, width):
    for axis, dim in sides:
        count = lax.axis_size(axis)
        forward = [(i, i + 1) for i in range(count - 1)]
        backward = [(target, source) for source, target in forward]
        low = lax.ppermute(
            lax.slice_in_dim(block, block.shape[dim] - width, None, axis=dim), axis, forward
        )
        high = lax.ppermute(lax.slice_in_dim(block, 0, width, axis=dim), axis, backward)
        block = jnp.concatenate([low, block, high], axis=dim)
    return block


def split_pair(values):
    high = values.astype(jnp.bfloat16)
    low = (values - high.astype(jnp.float32)).astype(jnp.bfloat16)
    return high, low


def stack_field(field):
    high_x, low_x = split_pair(field[0])
    high_y, low_y = split_pair(field[1])
    return jnp.concatenate([high_x, high_y, low_x, low_y], axis=0)


def column_onehot(low_ids, width):
    place = lax.broadcasted_iota(jnp.int32, (width, low_ids.shape[1]), 0)
    return jnp.where(place == low_ids, 1.0, 0.0).astype(jnp.bfloat16)


def row_mask(high_ids, rows):
    return lax.broadcasted_iota(jnp.int32, (rows, high_ids.shape[1]), 0) == high_ids


def pick(stacked, mask, onehot):
    rows = mask.shape[0]
    grown = jnp.dot(stacked, onehot, preferred_element_type=jnp.float32)
    both = grown[: 2 * rows] + grown[2 * rows :]
    value_x = jnp.sum(jnp.where(mask, both[:rows], 0.0), axis=0, keepdims=True)
    value_y = jnp.sum(jnp.where(mask, both[rows:], 0.0), axis=0, keepdims=True)
    return value_x, value_y


def masked_stack(mask, value_x, value_y):
    parts = split_f32(value_x, value_y)
    return jnp.concatenate(
        [jnp.where(mask, part, 0.0).astype(jnp.bfloat16) for part in parts], axis=0
    )


def split_f32(value_x, value_y):
    high_x = value_x.astype(jnp.bfloat16).astype(jnp.float32)
    high_y = value_y.astype(jnp.bfloat16).astype(jnp.float32)
    return high_x, high_y, value_x - high_x, value_y - high_y


def add_in(stacks, onehots):
    left = jnp.concatenate(stacks, axis=1)
    right = jnp.concatenate(onehots, axis=1)
    return lax.dot_general(
        left, right, (((1,), (1,)), ((), ())), preferred_element_type=jnp.float32
    )


def unstack(total):
    both = total[: total.shape[0] // 2] + total[total.shape[0] // 2 :]
    rows = both.shape[0] // 2
    return both[:rows], both[rows:]


def strain_rows(values, grad):
    value_x, value_y = values
    strain_xx = grad[0] * value_x[0] + grad[1] * value_x[1] + grad[2] * value_x[2]
    strain_yy = grad[3] * value_y[0] + grad[4] * value_y[1] + grad[5] * value_y[2]
    strain_xy = 0.5 * (
        (grad[3] * value_x[0] + grad[0] * value_y[0])
        + (grad[4] * value_x[1] + grad[1] * value_y[1])
        + (grad[5] * value_x[2] + grad[2] * value_y[2])
    )
    return strain_xx, strain_yy, strain_xy


def chunk_of(step):
    return pl.ds(pl.multiple_of(step * CHUNK, CHUNK), CHUNK)


def gather_chunk(stacked, high_ref, low_ref, cols, rows, width):
    masks, onehots, value_x, value_y = [], [], [], []
    for a in range(3):
        mask = row_mask(high_ref[a : a + 1, cols], rows)
        onehot = column_onehot(low_ref[a : a + 1, cols], width)
        got_x, got_y = pick(stacked, mask, onehot)
        masks.append(mask)
        onehots.append(onehot)
        value_x.append(got_x)
        value_y.append(got_y)
    return masks, onehots, (value_x, value_y)


def viscosity_loop(stack_ref, high_ref, low_ref, geom_ref, scale_ref, coef_ref, rows):
    width = stack_ref.shape[1]

    def body(step, carry):
        cols = chunk_of(step)
        _, _, values = gather_chunk(stack_ref[...], high_ref, low_ref, cols, rows, width)
        grad = [geom_ref[i : i + 1, cols] for i in range(6)]
        exx, eyy, exy = strain_rows(values, grad)
        effective = exx * exx + eyy * eyy + exx * eyy + exy * exy + STRAIN_FLOOR
        viscosity = 0.5 * GLEN_B * jnp.exp(jnp.log(effective) * (-1.0 / 3.0))
        coef_ref[:, cols] = 2.0 * viscosity * scale_ref[:, cols]
        return carry

    lax.fori_loop(0, high_ref.shape[1] // CHUNK, body, 0)


def operate_loop(stack_ref, high_ref, low_ref, geom_ref, coef_ref, total_ref, rows):
    width = stack_ref.shape[1]
    total_ref[...] = jnp.zeros_like(total_ref)

    def body(step, carry):
        cols = chunk_of(step)
        masks, onehots, values = gather_chunk(
            stack_ref[...], high_ref, low_ref, cols, rows, width
        )
        grad = [geom_ref[i : i + 1, cols] for i in range(6)]
        coefficient = coef_ref[:, cols]
        exx, eyy, exy = strain_rows(values, grad)
        sxx = coefficient * (2.0 * exx + eyy)
        syy = coefficient * (exx + 2.0 * eyy)
        sxy = coefficient * exy
        stacks = [
            masked_stack(
                masks[a],
                sxx * grad[a] + sxy * grad[3 + a],
                syy * grad[3 + a] + sxy * grad[a],
            )
            for a in range(3)
        ]
        total_ref[...] += add_in(stacks, onehots)
        return carry

    lax.fori_loop(0, high_ref.shape[1] // CHUNK, body, 0)


def read_loop(stack_ref, high_ref, low_ref, weight_x_ref, weight_y_ref, read_ref, rows):
    width = stack_ref.shape[1]

    def body(step, carry):
        cols = chunk_of(step)
        _, _, values = gather_chunk(stack_ref[...], high_ref, low_ref, cols, rows, width)
        total = 0.0
        for a in range(3):
            total = total + (
                weight_x_ref[a : a + 1, cols] * values[0][a]
                + weight_y_ref[a : a + 1, cols] * values[1][a]
            )
        read_ref[:, cols] = total
        return carry

    lax.fori_loop(0, high_ref.shape[1] // CHUNK, body, 0)


def spread_loop(arrived_ref, high_ref, low_ref, weight_x_ref, weight_y_ref, total_ref, rows):
    width = total_ref.shape[1]
    total_ref[...] = jnp.zeros_like(total_ref)

    def body(step, carry):
        cols = chunk_of(step)
        arrived = arrived_ref[:, cols]
        stacks, onehots = [], []
        for a in range(3):
            mask = row_mask(high_ref[a : a + 1, cols], rows)
            onehots.append(column_onehot(low_ref[a : a + 1, cols], width))
            stacks.append(
                masked_stack(
                    mask,
                    arrived * weight_x_ref[a : a + 1, cols],
                    arrived * weight_y_ref[a : a + 1, cols],
                )
            )
        total_ref[...] += add_in(stacks, onehots)
        return carry

    lax.fori_loop(0, high_ref.shape[1] // CHUNK, body, 0)


def viscosity_kernel(field_ref, high_ref, low_ref, geom_ref, scale_ref, coef_ref, stack_ref):
    stack_ref[...] = stack_field(field_ref)
    viscosity_loop(
        stack_ref, high_ref, low_ref, geom_ref, scale_ref, coef_ref, field_ref.shape[1]
    )


def operate_kernel(
    field_ref, high_ref, low_ref, geom_ref, coef_ref, out_ref, stack_ref, total_ref
):
    stack_ref[...] = stack_field(field_ref)
    operate_loop(
        stack_ref, high_ref, low_ref, geom_ref, coef_ref, total_ref, field_ref.shape[1]
    )
    out_ref[0], out_ref[1] = unstack(total_ref[...])


def read_kernel(field_ref, high_ref, low_ref, wx_ref, wy_ref, read_ref, stack_ref):
    stack_ref[...] = stack_field(field_ref)
    read_loop(stack_ref, high_ref, low_ref, wx_ref, wy_ref, read_ref, field_ref.shape[1])


def spread_kernel(arrived_ref, high_ref, low_ref, wx_ref, wy_ref, out_ref, total_ref):
    spread_loop(arrived_ref, high_ref, low_ref, wx_ref, wy_ref, total_ref, out_ref.shape[1])
    out_ref[0], out_ref[1] = unstack(total_ref[...])


def call(kernel, out, scratch, *args):
    return pl.pallas_call(
        kernel,
        out_shape=jax.ShapeDtypeStruct(out, jnp.float32),
        in_specs=[pl.BlockSpec(memory_space=pltpu.VMEM)] * len(args),
        out_specs=pl.BlockSpec(memory_space=pltpu.VMEM),
        scratch_shapes=scratch,
        compiler_params=pltpu.CompilerParams(vmem_limit_bytes=48 * 1024 * 1024),
    )(*args)


def split_ids(ids, node_rows, columns):
    row = ids // (columns + 2)
    col = ids % (columns + 2)
    left, right = col == 0, col == columns + 1
    high = jnp.where(left | right, node_rows + 2, row)
    low = jnp.where(left, row, jnp.where(right, row + RIM, col - 1))
    return high, low


def weigh_rows(readings, precision, couple):
    grid_read = readings.reshape(-1, 128)
    grid_prec = precision.reshape(-1, 128)
    grid_couple = couple.reshape(-1, 128)
    column = jnp.arange(128)[None, :]
    next_prec = jnp.concatenate([grid_prec[:, 1:], grid_prec[:, :1]], axis=1)
    link_weight = jnp.where(column < 127, grid_couple * jnp.sqrt(grid_prec * next_prec), 0.0)
    zero_col = jnp.zeros_like(grid_read[:, :1])
    next_read = jnp.concatenate([grid_read[:, 1:], zero_col], axis=1)
    prev_read = jnp.concatenate([zero_col, grid_read[:, :-1]], axis=1)
    prev_link = jnp.concatenate([zero_col, link_weight[:, :-1]], axis=1)
    return (grid_prec * grid_read - link_weight * next_read - prev_link * prev_read).reshape(-1)


def ghosted(field):
    return padded(field, (("wide", 1), ("narrow", 2)), 1)


def reduce_rims(summed):
    side_cols = jnp.concatenate([summed[:, :, :1], summed[:, :, -1:]], axis=2)
    beside = padded(side_cols, (("narrow", 2),), 1)
    middle = summed[:, :, 1:-1]
    middle = middle.at[:, :, 0].add(beside[:, :, 0]).at[:, :, -1].add(beside[:, :, 3])
    side_rows = jnp.concatenate([middle[:, :1], middle[:, -1:]], axis=1)
    across = padded(side_rows, (("wide", 1),), 1)
    interior = middle[:, 1:-1]
    return interior.at[:, 0].add(across[:, 0]).at[:, -1].add(across[:, 3])


def norm_sum(residual):
    return lax.psum(jnp.sum(residual * residual), ("wide", "narrow"))


def per_device(
    state_vel,
    friction,
    basal_area,
    direction_beta,
    elem_nodes,
    elem_geom,
    elem_thick,
    live_blocks,
    pix_dest,
    pix_prec,
    pix_couple,
    obs_nodes,
    obs_bary,
    obs_angle,
):
    node_rows, columns = friction.shape
    rows = -(-(node_rows + 3) // 8) * 8
    elements = elem_nodes.shape[1]
    core_index = lax.axis_index("sub")
    alive = jnp.arange(elements, dtype=jnp.int32) // 128 < live_blocks[core_index]
    scale = jnp.where(alive, elem_thick * elem_geom[6], 0.0)[None, :]
    high, low = split_ids(elem_nodes, node_rows, columns)
    obs_high, obs_low = split_ids(obs_nodes, node_rows, columns)
    basal_drag = jnp.exp(friction) * basal_area
    stack = pltpu.VMEM((4 * rows, columns), jnp.bfloat16)
    total = pltpu.VMEM((4 * rows, columns), jnp.float32)

    def spread(field):
        wide = ghosted(field)
        room = ((0, 0), (0, RIM - node_rows - 2))
        rim = jnp.concatenate([jnp.pad(wide[:, :, 0], room), jnp.pad(wide[:, :, -1], room)], axis=1)
        gap = jnp.zeros((2, rows - node_rows - 3, columns), jnp.float32)
        return jnp.concatenate([wide[:, :, 1:-1], rim[:, None, :], gap], axis=1)

    def finish(partial):
        both = lax.psum(partial, "sub")
        rim = both[:, node_rows + 2]
        left = rim[:, : node_rows + 2, None]
        right = rim[:, RIM : RIM + node_rows + 2, None]
        return reduce_rims(jnp.concatenate([left, both[:, : node_rows + 2], right], axis=2))

    coefficient = call(
        viscosity_kernel, (1, elements), [stack], spread(state_vel), high, low, elem_geom, scale
    )

    def operate(field):
        partial = call(
            operate_kernel,
            (2, rows, columns),
            [stack, total],
            spread(field),
            high,
            low,
            elem_geom,
            coefficient,
        )
        return finish(partial) + basal_drag * field

    def solve_field(right_side):
        solution = jnp.zeros_like(right_side)
        residual = right_side
        direction = right_side
        norm_now = norm_sum(residual)
        for iteration in range(CG_ITERS):
            applied = operate(direction)
            step_size = norm_now / lax.psum(jnp.sum(direction * applied), ("wide", "narrow"))
            solution = solution + step_size * direction
            residual = residual - step_size * applied
            if iteration + 1 < CG_ITERS:
                norm_next = norm_sum(residual)
                direction = residual + norm_next / norm_now * direction
                norm_now = norm_next
        return solution

    owners = lax.axis_size(("wide", "narrow"))
    capacity = obs_angle.shape[0] // owners
    tangent_vel = solve_field(-basal_drag * direction_beta * state_vel)
    weight_x = obs_bary * jnp.cos(obs_angle)
    weight_y = obs_bary * jnp.sin(obs_angle)
    readings = call(
        read_kernel,
        (1, obs_angle.shape[0]),
        [stack],
        spread(tangent_vel),
        obs_high,
        obs_low,
        weight_x,
        weight_y,
    ).reshape(owners, capacity)
    returned = lax.all_to_all(readings, ("wide", "narrow"), split_axis=0, concat_axis=0, tiled=True)
    target = pix_dest[:, 0]
    onehot = (target[:, None] == jnp.arange(owners, dtype=jnp.int32)[None, :]).astype(jnp.int32)
    running = jnp.cumsum(onehot, axis=0, dtype=jnp.int32)
    slot_rank = jnp.sum(jnp.where(onehot == 1, running, 0), axis=1) - 1
    slot_index = target * capacity + slot_rank
    weighted = weigh_rows(returned.reshape(-1)[slot_index], pix_prec, pix_couple)
    outgoing = (
        jnp.zeros((owners * capacity,), jnp.float32)
        .at[slot_index]
        .set(weighted)
        .reshape(owners, capacity)
    )
    arrived = lax.all_to_all(outgoing, ("wide", "narrow"), split_axis=0, concat_axis=0, tiled=True)
    partial = call(
        spread_kernel,
        (2, rows, columns),
        [total],
        arrived.reshape(1, -1),
        obs_high,
        obs_low,
        weight_x,
        weight_y,
    )
    adjoint = solve_field(finish(partial))
    hess_vec = -basal_drag * (state_vel[0] * adjoint[0] + state_vel[1] * adjoint[1])
    return (tangent_vel, hess_vec)


def node_ids(ids, node_rows, columns):
    row = ids // (columns + 2)
    col = ids % (columns + 2)
    left, right = col == 0, col == columns + 1
    inner = jnp.where(row == 0, node_rows, jnp.where(row == node_rows + 1, row, row - 1))
    high = jnp.where(left | right, node_rows + 2, inner)
    low = jnp.where(left, row, jnp.where(right, row + RIM, col - 1))
    return high, low


SCALE = 12


def shared_chunk(stack_ref, work_ref, cols, rows):
    width = stack_ref.shape[1]
    ids = work_ref[0:6, cols].astype(jnp.int32)
    masks, onehots, value_x, value_y = [], [], [], []
    for a in range(3):
        masks.append(row_mask(ids[a : a + 1], rows))
        onehots.append(column_onehot(ids[3 + a : 4 + a], width))
        got_x, got_y = pick(stack_ref[...], masks[a], onehots[a])
        value_x.append(got_x)
        value_y.append(got_y)
    grad = [work_ref[6 + i : 7 + i, cols] for i in range(6)]
    return masks, onehots, grad, strain_rows((value_x, value_y), grad)


def shared_viscosity(stack_ref, work_ref, coef_ref, rows):
    def body(step, carry):
        cols = chunk_of(step)
        _, _, _, (exx, eyy, exy) = shared_chunk(stack_ref, work_ref, cols, rows)
        effective = exx * exx + eyy * eyy + exx * eyy + exy * exy + STRAIN_FLOOR
        viscosity = 0.5 * GLEN_B * jnp.exp(jnp.log(effective) * (-1.0 / 3.0))
        coef_ref[:, cols] = 2.0 * viscosity * work_ref[SCALE : SCALE + 1, cols]
        return carry

    lax.fori_loop(0, work_ref.shape[1] // CHUNK, body, 0, unroll=2)


def shared_operate(stack_ref, work_ref, coef_ref, total_ref, rows):
    total_ref[...] = jnp.zeros_like(total_ref)

    def body(step, carry):
        total = total_ref[...]
        parts = []
        for half in range(2):
            cols = chunk_of(2 * step + half)
            masks, onehots, grad, strain = shared_chunk(stack_ref, work_ref, cols, rows)
            exx, eyy, exy = strain
            coefficient = coef_ref[:, cols]
            sxx = coefficient * (2.0 * exx + eyy)
            syy = coefficient * (exx + 2.0 * eyy)
            sxy = coefficient * exy
            stacks = [
                masked_stack(
                    masks[a],
                    sxx * grad[a] + sxy * grad[3 + a],
                    syy * grad[3 + a] + sxy * grad[a],
                )
                for a in range(3)
            ]
            parts.append((stacks, onehots))
        for stacks, onehots in parts:
            total = total + add_in(stacks, onehots)
        total_ref[...] = total
        return carry

    lax.fori_loop(0, work_ref.shape[1] // (2 * CHUNK), body, 0)


SIDES = [(dw, dn) for dw in (-1, 0, 1) for dn in (-1, 0, 1)]
TILE = 8


def whole_kernel(
    wide,
    narrow,
    state_ref,
    friction_ref,
    area_ref,
    beta_ref,
    packed_ref,
    live_ref,
    dest_ref,
    prec_ref,
    couple_ref,
    obs_high_ref,
    obs_low_ref,
    wx_ref,
    wy_ref,
    tangent_ref,
    hess_ref,
    stack_ref,
    total_ref,
    coef_ref,
    drag_ref,
    vel_ref,
    p_ref,
    r_ref,
    x_ref,
    q_ref,
    field_send,
    field_recv,
    rim_send,
    rim_recv,
    sum_send,
    sum_recv,
    pix_send,
    pix_recv,
    other_ref,
    work_ref,
    other_sems,
    field_ss,
    field_rs,
    rim_ss,
    rim_rs,
    sum_ss,
    sum_rs,
    pix_ss,
    pix_rs,
):
    node_rows, columns = friction_ref.shape
    rows = vel_ref.shape[1]
    count = wide * narrow
    my_w = lax.axis_index("wide")
    my_n = lax.axis_index("narrow")
    my_s = lax.axis_index("sub")
    me = my_w * narrow + my_n
    f32 = jnp.float32

    def place_of(q):
        return {"wide": q // narrow, "narrow": lax.rem(q, narrow), "sub": my_s}

    partner = {"wide": my_w, "narrow": my_n, "sub": 1 - my_s}
    barrier = pltpu.get_barrier_semaphore()
    pl.semaphore_signal(barrier, inc=1, device_id=partner, device_id_type=pl.DeviceIdType.MESH)
    for k in range(1, count):
        pl.semaphore_signal(
            barrier,
            inc=1,
            device_id=place_of(lax.rem(me + k, count)),
            device_id_type=pl.DeviceIdType.MESH,
        )
    pl.semaphore_wait(barrier, count)

    trade = pltpu.make_async_remote_copy(
        src_ref=packed_ref,
        dst_ref=other_ref,
        send_sem=other_sems.at[0],
        recv_sem=other_sems.at[1],
        device_id=partner,
        device_id_type=pl.DeviceIdType.MESH,
    )
    trade.start()
    row_at = lax.broadcasted_iota(jnp.int32, (rows, columns), 0)
    lane_at = lax.broadcasted_iota(jnp.int32, (rows, columns), 1)
    eye_row = lax.broadcasted_iota(jnp.int32, (rows, RIM), 0)
    eye_lane = lax.broadcasted_iota(jnp.int32, (rows, RIM), 1)
    eye_row = jnp.where(
        eye_row < node_rows,
        eye_row + 1,
        jnp.where(eye_row == node_rows, 0, jnp.where(eye_row == node_rows + 1, eye_row, -1)),
    )
    eye = eye_row == eye_lane
    rim_lane = lax.broadcasted_iota(jnp.int32, (1, RIM), 1)

    def exists(dw, dn):
        w, n = my_w + dw, my_n + dn
        return (w >= 0) & (w < wide) & (n >= 0) & (n < narrow)

    has_up, has_down = my_w > 0, my_w < wide - 1
    has_left, has_right = my_n > 0, my_n < narrow - 1
    rim_row = jnp.where(lane_at >= RIM, lane_at - RIM, lane_at)
    rim_side = ((lane_at < RIM) & has_left) | ((lane_at >= RIM) & has_right)
    rim_in = (
        ((rim_row >= 1) & (rim_row <= node_rows))
        | ((rim_row == 0) & has_up)
        | ((rim_row == node_rows + 1) & has_down)
    )
    inside = (
        (row_at < node_rows)
        | ((row_at == node_rows) & has_up)
        | ((row_at == node_rows + 1) & has_down)
        | ((row_at == node_rows + 2) & rim_side & rim_in)
    )

    def col_lanes(field, lane):
        column = field[:, lane : lane + 1]
        return jnp.sum(jnp.where(eye, column, 0.0), axis=0, keepdims=True)

    def lanes_col(lanes):
        return jnp.sum(jnp.where(eye, lanes, 0.0), axis=1, keepdims=True)

    def rim_copy(k, slot):
        dw, dn = SIDES[slot]
        return pltpu.make_async_remote_copy(
            src_ref=rim_send.at[k],
            dst_ref=rim_recv.at[k, 8 - slot],
            send_sem=rim_ss.at[k, slot],
            recv_sem=rim_rs.at[k, 8 - slot],
            device_id={"wide": my_w + dw, "narrow": my_n + dn, "sub": my_s},
            device_id_type=pl.DeviceIdType.MESH,
        )

    def rim_landed(k, slot):
        dw, dn = SIDES[slot]
        return pltpu.make_async_remote_copy(
            src_ref=rim_send.at[k],
            dst_ref=rim_recv.at[k, slot],
            send_sem=rim_ss.at[k, slot],
            recv_sem=rim_rs.at[k, slot],
            device_id={"wide": my_w + dw, "narrow": my_n + dn, "sub": my_s},
            device_id_type=pl.DeviceIdType.MESH,
        )

    def rim_start(k, fields):
        lines = []
        for at in (node_rows, 0, node_rows - 1, node_rows + 1, node_rows + 2):
            lines += [field[at : at + 1] for field in fields]
        lines += [
            jnp.concatenate([col_lanes(field, 0), col_lanes(field, columns - 1)], axis=1)
            for field in fields
        ]
        for i, line in enumerate(lines):
            rim_send[k, i : i + 1, :] = line
        for slot, side in enumerate(SIDES):
            if side != (0, 0):

                @pl.when(exists(*side))
                def _():
                    rim_copy(k, slot).start()

    def moved(lanes, dw):
        if dw == 0:
            return lanes
        if dw < 0:
            turned = pltpu.roll(lanes, (RIM - node_rows) % RIM, 1)
            return jnp.where(rim_lane < 2, turned, 0.0)
        turned = pltpu.roll(lanes, node_rows, 1)
        keep = (rim_lane == node_rows) | (rim_lane == node_rows + 1)
        return jnp.where(keep, turned, 0.0)

    def rim_finish(k, fields):
        for slot, side in enumerate(SIDES):
            if side != (0, 0):

                @pl.when(exists(*side))
                def _():
                    rim_landed(k, slot).wait_recv()
                    rim_landed(k, slot).wait_send()

        done = []
        for c, field in enumerate(fields):

            def got(dw, dn, line, low, size):
                slot = SIDES.index((dw, dn))
                at = 2 * line + c
                value = rim_recv[k, slot, at : at + 1, low : low + size]
                return jnp.where(exists(dw, dn), value, 0.0)

            left_rim = jnp.zeros((1, RIM), f32)
            right_rim = jnp.zeros((1, RIM), f32)
            left_col = jnp.zeros((1, RIM), f32)
            right_col = jnp.zeros((1, RIM), f32)
            for dw in (-1, 1):
                left_rim = left_rim + moved(got(dw, 0, 4, 0, RIM), dw)
                right_rim = right_rim + moved(got(dw, 0, 4, RIM, RIM), dw)
            for dw in (0, -1, 1):
                left_col = left_col + moved(got(dw, -1, 4, RIM, RIM), dw)
                left_rim = left_rim + moved(got(dw, -1, 5, RIM, RIM), dw)
                right_col = right_col + moved(got(dw, 1, 4, 0, RIM), dw)
                right_rim = right_rim + moved(got(dw, 1, 5, 0, RIM), dw)
            result = field
            for at, dw, line in (
                (node_rows, -1, 2),
                (0, -1, 3),
                (node_rows - 1, 1, 0),
                (node_rows + 1, 1, 1),
            ):
                result = result + jnp.where(row_at == at, got(dw, 0, line, 0, columns), 0.0)
            rim = jnp.concatenate([left_rim, right_rim], axis=1)
            result = result + jnp.where(row_at == node_rows + 2, rim, 0.0)
            result = result + jnp.where(lane_at == 0, lanes_col(left_col), 0.0)
            result = result + jnp.where(lane_at == columns - 1, lanes_col(right_col), 0.0)
            done.append(jnp.where(inside, result, 0.0))
        return done

    def all_copy(send, recv, ss, rs, k, target, slot):
        return pltpu.make_async_remote_copy(
            src_ref=send,
            dst_ref=recv.at[k, slot],
            send_sem=ss.at[k, target],
            recv_sem=rs.at[k, slot],
            device_id=place_of(target),
            device_id_type=pl.DeviceIdType.MESH,
        )

    def sum_start(k, *values):
        for i, value in enumerate(values):
            sum_send[k, i : i + 1, :] = jnp.broadcast_to(value, (1, 128))
        for j in range(1, count):
            q = lax.rem(me + j, count)
            all_copy(sum_send.at[k], sum_recv, sum_ss, sum_rs, k, q, me).start()
        sum_recv[k, me] = sum_send[k]

    def sum_finish(k):
        for j in range(1, count):
            q = lax.rem(me + j, count)
            copy = all_copy(sum_send.at[k], sum_recv, sum_ss, sum_rs, k, q, q)
            copy.wait_recv()
            copy.wait_send()
        total = sum_recv[k, 0]
        for q in range(1, count):
            total = total + sum_recv[k, q]
        return total[0:1, 0:1], total[1:2, 0:1]

    def pix_trade(k):
        for j in range(1, count):
            q = lax.rem(me + j, count)
            all_copy(pix_send.at[k, q], pix_recv, pix_ss, pix_rs, k, q, me).start()
        pix_recv[k, me] = pix_send[k, me]
        for j in range(1, count):
            q = lax.rem(me + j, count)
            copy = all_copy(pix_send.at[k, q], pix_recv, pix_ss, pix_rs, k, q, q)
            copy.wait_recv()
            copy.wait_send()

    def core_sum(k):
        field_send[k, 0], field_send[k, 1] = unstack(total_ref[...])
        copy = pltpu.make_async_remote_copy(
            src_ref=field_send.at[k],
            dst_ref=field_recv.at[k],
            send_sem=field_ss.at[k],
            recv_sem=field_rs.at[k],
            device_id=partner,
            device_id_type=pl.DeviceIdType.MESH,
        )
        copy.start()
        copy.wait()
        return [field_send[k, c] + field_recv[k, c] for c in range(2)]

    def dot(a, b):
        down = jnp.sum(a * b, axis=0, keepdims=True)
        return jnp.sum(down, axis=1, keepdims=True)

    def both(a_ref, b_ref, size):
        return dot(a_ref[0, :size], b_ref[0, :size]) + dot(a_ref[1, :size], b_ref[1, :size])

    def solve(field_at, rim_at, sum_at):
        for c in range(2):
            p_ref[c] = r_ref[c]
        norm_now = None
        for step in range(CG_ITERS):
            stack_ref[...] = stack_field(p_ref)
            shared_operate(stack_ref, work_ref, coef_ref, total_ref, rows)
            local = core_sum(field_at + step)
            rim_start(rim_at + step, local)
            energy = dot(local[0], p_ref[0]) + dot(local[1], p_ref[1])
            for c in range(2):
                field = p_ref[c, :node_rows]
                energy = energy + dot(drag_ref[:node_rows] * field, field)
            norm = both(r_ref, r_ref, node_rows)
            sum_start(sum_at + 2 * step, norm, energy)
            applied = rim_finish(rim_at + step, local)
            for c in range(2):
                q_ref[c] = applied[c] + drag_ref[...] * p_ref[c]
            norm_now, energy = sum_finish(sum_at + 2 * step)
            alpha = norm_now / energy
            for c in range(2):
                if step == 0:
                    x_ref[c] = alpha * p_ref[c]
                else:
                    x_ref[c] = x_ref[c] + alpha * p_ref[c]
            if step + 1 < CG_ITERS:
                for c in range(2):
                    r_ref[c] = r_ref[c] - alpha * q_ref[c]
                norm = both(r_ref, r_ref, node_rows)
                sum_start(sum_at + 2 * step + 1, norm)
                norm_next, _ = sum_finish(sum_at + 2 * step + 1)
                ratio = norm_next / norm_now
                for c in range(2):
                    p_ref[c] = r_ref[c] + ratio * p_ref[c]

    sum_send[...] = jnp.zeros_like(sum_send)
    rim_send[...] = jnp.zeros_like(rim_send)
    pix_send[...] = jnp.zeros_like(pix_send)
    gap = jnp.zeros((rows - node_rows, columns), f32)

    def grown(value):
        return jnp.concatenate([value, gap], axis=0)

    vel = [grown(state_ref[0]), grown(state_ref[1])]
    rim_start(0, vel)
    other = [grown(jnp.exp(friction_ref[...]) * area_ref[...]), grown(beta_ref[...])]
    rim_start(1, other)
    vel_ref[0], vel_ref[1] = rim_finish(0, vel)
    drag, beta = rim_finish(1, other)
    drag_ref[...] = drag
    for c in range(2):
        r_ref[c] = -drag * beta * vel_ref[c]
    stack_ref[...] = stack_field(vel_ref)
    trade.wait()
    share = work_ref.shape[1] // 128
    blocks = packed_ref.shape[0]
    first_live = live_ref[0]
    all_live = first_live + live_ref[1]

    def take(i, carry):
        position = my_s * share + i
        of_first = position < first_live
        at = jnp.where(
            of_first, jnp.minimum(position, blocks - 1), jnp.clip(position - first_live, 0, blocks - 1)
        )
        mine = jnp.where(of_first, 1, 0) + my_s == 1
        block = jnp.where(mine, packed_ref[at], other_ref[at])
        alive = (position < all_live) | (piece_row < SCALE)
        cols = pl.ds(pl.multiple_of(i * 128, 128), 128)
        work_ref[:, cols] = jnp.where(alive, block, 0.0)
        return carry

    piece_row = lax.broadcasted_iota(jnp.int32, (16, 128), 0)
    lax.fori_loop(0, share, take, 0)
    shared_viscosity(stack_ref, work_ref, coef_ref, rows)
    solve(0, 2, 0)
    tangent_ref[...] = x_ref[:, :node_rows]

    capacity = obs_high_ref.shape[1] // count
    lines = capacity // 128
    stack_ref[...] = stack_field(x_ref)

    def read(step, carry):
        cols = pl.ds(pl.multiple_of(step * capacity, 128), capacity)
        _, _, values = gather_chunk(
            stack_ref[...], obs_high_ref, obs_low_ref, cols, rows, columns
        )
        total = jnp.zeros((1, capacity), f32)
        for a in range(3):
            total = total + (
                wx_ref[a : a + 1, cols] * values[0][a] + wy_ref[a : a + 1, cols] * values[1][a]
            )
        for j in range(lines):
            pix_send[0, step, j : j + 1, :] = total[:, j * 128 : (j + 1) * 128]
        return carry

    lax.fori_loop(0, count, read, 0, unroll=2)
    pix_trade(0)

    dest = dest_ref[...]
    pixel_rows = dest.shape[0]
    named = jnp.concatenate(
        [jnp.where(dest == q, 1.0, 0.0) for q in range(count)], axis=0
    ).astype(jnp.bfloat16)
    first = lax.broadcasted_iota(jnp.int32, (128, 128), 0)
    second = lax.broadcasted_iota(jnp.int32, (128, 128), 1)
    before = jnp.where(first < second, 1.0, 0.0).astype(jnp.bfloat16)
    ones = jnp.ones((128, 128), jnp.bfloat16)
    within = jnp.dot(named, before, preferred_element_type=f32)
    per_row = jnp.dot(named, ones, preferred_element_type=f32).astype(jnp.bfloat16)
    size = count * pixel_rows
    first = lax.broadcasted_iota(jnp.int32, (size, size), 0)
    second = lax.broadcasted_iota(jnp.int32, (size, size), 1)
    start = first // pixel_rows * pixel_rows
    above = jnp.where((second >= start) & (second < first), 1.0, 0.0).astype(jnp.bfloat16)
    ranks = within + jnp.dot(above, per_row, preferred_element_type=f32)
    rank = jnp.zeros((pixel_rows, 128), f32)
    for q in range(count):
        rank = rank + jnp.where(dest == q, ranks[q * pixel_rows : (q + 1) * pixel_rows], 0.0)
    rank = rank.astype(jnp.int32)
    slot_line = dest * TILE + rank // 128
    slot_lane = lax.rem(rank, 128)

    def flat(value):
        return jnp.concatenate([value[i : i + 1] for i in range(pixel_rows)], axis=1)

    table = count * TILE
    line_mask = row_mask(flat(slot_line), table)
    lane_hot = column_onehot(flat(slot_lane), 128)
    high, low = split_pair(pix_recv[0].reshape(table, 128))
    spread_out = jnp.dot(
        jnp.concatenate([high, low], axis=0), lane_hot, preferred_element_type=f32
    )
    spread_out = spread_out[:table] + spread_out[table:]
    line = jnp.sum(jnp.where(line_mask, spread_out, 0.0), axis=0, keepdims=True)
    reading = jnp.concatenate(
        [line[:, i * 128 : (i + 1) * 128] for i in range(pixel_rows)], axis=0
    )
    precision = prec_ref[...]
    column = lax.broadcasted_iota(jnp.int32, (pixel_rows, 128), 1)
    link = jnp.where(
        column < 127,
        couple_ref[...] * jnp.sqrt(precision * pltpu.roll(precision, 127, 1)),
        0.0,
    )
    weighted = (
        precision * reading
        - link * pltpu.roll(reading, 127, 1)
        - pltpu.roll(link, 1, 1) * pltpu.roll(reading, 1, 1)
    )
    weighted = flat(weighted)
    top = weighted.astype(jnp.bfloat16).astype(f32)
    left = jnp.concatenate(
        [jnp.where(line_mask, part, 0.0).astype(jnp.bfloat16) for part in (top, weighted - top)],
        axis=0,
    )
    out = lax.dot_general(
        left, lane_hot, (((1,), (1,)), ((), ())), preferred_element_type=f32
    )
    pix_send[1] = (out[:table] + out[table:]).reshape(count, TILE, 128)
    pix_trade(1)

    total_ref[...] = jnp.zeros_like(total_ref)

    def scatter(step, carry):
        cols = pl.ds(pl.multiple_of(step * capacity, 128), capacity)
        tile = pix_recv[1, step]
        arrived = jnp.concatenate([tile[j : j + 1] for j in range(lines)], axis=1)
        stacks, onehots = [], []
        for a in range(3):
            mask = row_mask(obs_high_ref[a : a + 1, cols], rows)
            onehots.append(column_onehot(obs_low_ref[a : a + 1, cols], columns))
            stacks.append(
                masked_stack(
                    mask, arrived * wx_ref[a : a + 1, cols], arrived * wy_ref[a : a + 1, cols]
                )
            )
        total_ref[...] += add_in(stacks, onehots)
        return carry

    lax.fori_loop(0, count, scatter, 0, unroll=2)
    local = core_sum(2)
    rim_start(4, local)
    r_ref[0], r_ref[1] = rim_finish(4, local)
    solve(3, 5, 3)
    hess_ref[...] = -drag_ref[:node_rows] * (
        state_ref[0] * x_ref[0, :node_rows] + state_ref[1] * x_ref[1, :node_rows]
    )


def fused_device(
    state_vel,
    friction,
    basal_area,
    direction_beta,
    elem_nodes,
    elem_geom,
    elem_thick,
    live_blocks,
    pix_dest,
    pix_prec,
    pix_couple,
    obs_nodes,
    obs_bary,
    obs_angle,
):
    node_rows, columns = friction.shape
    rows = -(-(node_rows + 3) // 8) * 8
    elements = elem_nodes.shape[1]
    wide, narrow = lax.axis_size("wide"), lax.axis_size("narrow")
    count = wide * narrow
    alive = jnp.arange(elements, dtype=jnp.int32) // 128 < live_blocks[lax.axis_index("sub")]
    scale = jnp.where(alive, elem_thick * elem_geom[6], 0.0)[None, :]
    high, low = node_ids(elem_nodes, node_rows, columns)
    packed = jnp.concatenate(
        [
            high.astype(jnp.float32),
            low.astype(jnp.float32),
            elem_geom[0:6],
            scale,
            jnp.zeros((3, elements), jnp.float32),
        ],
        axis=0,
    )
    packed = packed.reshape(16, -1, 128).transpose(1, 0, 2)
    share = 2 * (elements // 128) // 3
    obs_high, obs_low = node_ids(obs_nodes, node_rows, columns)
    weight_x = obs_bary * jnp.cos(obs_angle)
    weight_y = obs_bary * jnp.sin(obs_angle)
    f32 = jnp.float32
    pair = pltpu.VMEM((2, rows, columns), f32)
    args = (
        state_vel,
        friction,
        basal_area,
        direction_beta,
        packed,
        live_blocks,
        pix_dest.reshape(-1, 128),
        pix_prec.reshape(-1, 128),
        pix_couple.reshape(-1, 128),
        obs_high,
        obs_low,
        weight_x,
        weight_y,
    )
    dma = pltpu.SemaphoreType.DMA
    return pl.pallas_call(
        functools.partial(whole_kernel, wide, narrow),
        out_shape=(
            jax.ShapeDtypeStruct((2, node_rows, columns), f32),
            jax.ShapeDtypeStruct((node_rows, columns), f32),
        ),
        in_specs=[
            pl.BlockSpec(memory_space=pltpu.SMEM if arg is live_blocks else pltpu.VMEM)
            for arg in args
        ],
        out_specs=(pl.BlockSpec(memory_space=pltpu.VMEM),) * 2,
        scratch_shapes=[
            pltpu.VMEM((4 * rows, columns), jnp.bfloat16),
            pltpu.VMEM((4 * rows, columns), f32),
            pltpu.VMEM((1, share * 128), f32),
            pltpu.VMEM((rows, columns), f32),
            pair,
            pair,
            pair,
            pair,
            pair,
            pltpu.VMEM((5, 2, rows, columns), f32),
            pltpu.VMEM((5, 2, rows, columns), f32),
            pltpu.VMEM((7, 16, columns), f32),
            pltpu.VMEM((7, 9, 16, columns), f32),
            pltpu.VMEM((6, 8, 128), f32),
            pltpu.VMEM((6, count, 8, 128), f32),
            pltpu.VMEM((2, count, TILE, 128), f32),
            pltpu.VMEM((2, count, TILE, 128), f32),
            pltpu.VMEM(packed.shape, f32),
            pltpu.VMEM((16, share * 128), f32),
            dma((2,)),
            dma((5,)),
            dma((5,)),
            dma((7, 9)),
            dma((7, 9)),
            dma((6, count)),
            dma((6, count)),
            dma((2, count)),
            dma((2, count)),
        ],
        compiler_params=pltpu.CompilerParams(
            collective_id=0, has_side_effects=True, vmem_limit_bytes=48 * 1024 * 1024
        ),
    )(*args)


def choose(*args):
    count = lax.axis_size("wide") * lax.axis_size("narrow")
    capacity = args[-1].shape[0] // count
    columns = args[1].shape[1]
    share = 2 * (args[4].shape[1] // 128) // 3
    fits = share * 128 % (2 * CHUNK) == 0 and count % 2 == 0
    if fits and capacity % 128 == 0 and capacity <= 128 * TILE and columns == 2 * RIM and args[1].shape[0] + 2 <= RIM:
        return fused_device(*args)
    return per_device(*args)


def solution(mesh):
    placed = (
        P(None, ("groups", "wide"), "narrow"),
        P(("groups", "wide"), "narrow"),
        P(("groups", "wide"), "narrow"),
        P(("groups", "wide"), "narrow"),
        P(None, ("groups", "wide", "narrow", "sub")),
        P(None, ("groups", "wide", "narrow", "sub")),
        P(("groups", "wide", "narrow", "sub")),
        P(("groups", "wide", "narrow")),
        P(("groups", "wide", "narrow", "sub"), None),
        P(("groups", "wide", "narrow", "sub")),
        P(("groups", "wide", "narrow", "sub")),
        P(None, ("groups", "wide", "narrow", "sub")),
        P(None, ("groups", "wide", "narrow", "sub")),
        P(("groups", "wide", "narrow", "sub")),
    )
    return jax.shard_map(
        choose,
        mesh=mesh,
        in_specs=placed,
        out_specs=(P(None, ("groups", "wide"), "narrow"), P(("groups", "wide"), "narrow")),
        check_vma=False,
    )
```

```python
import functools

import jax
import jax.numpy as jnp
from jax import lax
from jax.experimental import pallas as pl
from jax.experimental.pallas import tpu as pltpu
from jax.sharding import PartitionSpec as P

CG_ITERS = 2

GLEN_B = 1.0
STRAIN_FLOOR = 0.01
RIM = 128
CHUNK = 512


def padded(block, sides, width):
    for axis, dim in sides:
        count = lax.axis_size(axis)
        forward = [(i, i + 1) for i in range(count - 1)]
        backward = [(target, source) for source, target in forward]
        low = lax.ppermute(
            lax.slice_in_dim(block, block.shape[dim] - width, None, axis=dim), axis, forward
        )
        high = lax.ppermute(lax.slice_in_dim(block, 0, width, axis=dim), axis, backward)
        block = jnp.concatenate([low, block, high], axis=dim)
    return block


def split_pair(values):
    high = values.astype(jnp.bfloat16)
    low = (values - high.astype(jnp.float32)).astype(jnp.bfloat16)
    return high, low


def stack_field(field):
    high_x, low_x = split_pair(field[0])
    high_y, low_y = split_pair(field[1])
    return jnp.concatenate([high_x, high_y, low_x, low_y], axis=0)


def column_onehot(low_ids, width):
    place = lax.broadcasted_iota(jnp.int32, (width, low_ids.shape[1]), 0)
    return jnp.where(place == low_ids, 1.0, 0.0).astype(jnp.bfloat16)


def row_mask(high_ids, rows):
    return lax.broadcasted_iota(jnp.int32, (rows, high_ids.shape[1]), 0) == high_ids


def pick(stacked, mask, onehot):
    rows = mask.shape[0]
    grown = jnp.dot(stacked, onehot, preferred_element_type=jnp.float32)
    both = grown[: 2 * rows] + grown[2 * rows :]
    value_x = jnp.sum(jnp.where(mask, both[:rows], 0.0), axis=0, keepdims=True)
    value_y = jnp.sum(jnp.where(mask, both[rows:], 0.0), axis=0, keepdims=True)
    return value_x, value_y


def masked_stack(mask, value_x, value_y):
    parts = split_f32(value_x, value_y)
    return jnp.concatenate(
        [jnp.where(mask, part, 0.0).astype(jnp.bfloat16) for part in parts], axis=0
    )


def split_f32(value_x, value_y):
    high_x = value_x.astype(jnp.bfloat16).astype(jnp.float32)
    high_y = value_y.astype(jnp.bfloat16).astype(jnp.float32)
    return high_x, high_y, value_x - high_x, value_y - high_y


def add_in(stacks, onehots):
    left = jnp.concatenate(stacks, axis=1)
    right = jnp.concatenate(onehots, axis=1)
    return lax.dot_general(
        left, right, (((1,), (1,)), ((), ())), preferred_element_type=jnp.float32
    )


def unstack(total):
    both = total[: total.shape[0] // 2] + total[total.shape[0] // 2 :]
    rows = both.shape[0] // 2
    return both[:rows], both[rows:]


def strain_rows(values, grad):
    value_x, value_y = values
    strain_xx = grad[0] * value_x[0] + grad[1] * value_x[1] + grad[2] * value_x[2]
    strain_yy = grad[3] * value_y[0] + grad[4] * value_y[1] + grad[5] * value_y[2]
    strain_xy = 0.5 * (
        (grad[3] * value_x[0] + grad[0] * value_y[0])
        + (grad[4] * value_x[1] + grad[1] * value_y[1])
        + (grad[5] * value_x[2] + grad[2] * value_y[2])
    )
    return strain_xx, strain_yy, strain_xy


def chunk_of(step):
    return pl.ds(pl.multiple_of(step * CHUNK, CHUNK), CHUNK)


def gather_chunk(stacked, high_ref, low_ref, cols, rows, width):
    masks, onehots, value_x, value_y = [], [], [], []
    for a in range(3):
        mask = row_mask(high_ref[a : a + 1, cols], rows)
        onehot = column_onehot(low_ref[a : a + 1, cols], width)
        got_x, got_y = pick(stacked, mask, onehot)
        masks.append(mask)
        onehots.append(onehot)
        value_x.append(got_x)
        value_y.append(got_y)
    return masks, onehots, (value_x, value_y)


def viscosity_loop(stack_ref, high_ref, low_ref, geom_ref, scale_ref, coef_ref, rows):
    width = stack_ref.shape[1]

    def body(step, carry):
        cols = chunk_of(step)
        _, _, values = gather_chunk(stack_ref[...], high_ref, low_ref, cols, rows, width)
        grad = [geom_ref[i : i + 1, cols] for i in range(6)]
        exx, eyy, exy = strain_rows(values, grad)
        effective = exx * exx + eyy * eyy + exx * eyy + exy * exy + STRAIN_FLOOR
        viscosity = 0.5 * GLEN_B * jnp.exp(jnp.log(effective) * (-1.0 / 3.0))
        coef_ref[:, cols] = 2.0 * viscosity * scale_ref[:, cols]
        return carry

    lax.fori_loop(0, high_ref.shape[1] // CHUNK, body, 0)


def operate_loop(stack_ref, high_ref, low_ref, geom_ref, coef_ref, total_ref, rows):
    width = stack_ref.shape[1]
    total_ref[...] = jnp.zeros_like(total_ref)

    def body(step, carry):
        cols = chunk_of(step)
        masks, onehots, values = gather_chunk(
            stack_ref[...], high_ref, low_ref, cols, rows, width
        )
        grad = [geom_ref[i : i + 1, cols] for i in range(6)]
        coefficient = coef_ref[:, cols]
        exx, eyy, exy = strain_rows(values, grad)
        sxx = coefficient * (2.0 * exx + eyy)
        syy = coefficient * (exx + 2.0 * eyy)
        sxy = coefficient * exy
        stacks = [
            masked_stack(
                masks[a],
                sxx * grad[a] + sxy * grad[3 + a],
                syy * grad[3 + a] + sxy * grad[a],
            )
            for a in range(3)
        ]
        total_ref[...] += add_in(stacks, onehots)
        return carry

    lax.fori_loop(0, high_ref.shape[1] // CHUNK, body, 0)


def read_loop(stack_ref, high_ref, low_ref, weight_x_ref, weight_y_ref, read_ref, rows):
    width = stack_ref.shape[1]

    def body(step, carry):
        cols = chunk_of(step)
        _, _, values = gather_chunk(stack_ref[...], high_ref, low_ref, cols, rows, width)
        total = 0.0
        for a in range(3):
            total = total + (
                weight_x_ref[a : a + 1, cols] * values[0][a]
                + weight_y_ref[a : a + 1, cols] * values[1][a]
            )
        read_ref[:, cols] = total
        return carry

    lax.fori_loop(0, high_ref.shape[1] // CHUNK, body, 0)


def spread_loop(arrived_ref, high_ref, low_ref, weight_x_ref, weight_y_ref, total_ref, rows):
    width = total_ref.shape[1]
    total_ref[...] = jnp.zeros_like(total_ref)

    def body(step, carry):
        cols = chunk_of(step)
        arrived = arrived_ref[:, cols]
        stacks, onehots = [], []
        for a in range(3):
            mask = row_mask(high_ref[a : a + 1, cols], rows)
            onehots.append(column_onehot(low_ref[a : a + 1, cols], width))
            stacks.append(
                masked_stack(
                    mask,
                    arrived * weight_x_ref[a : a + 1, cols],
                    arrived * weight_y_ref[a : a + 1, cols],
                )
            )
        total_ref[...] += add_in(stacks, onehots)
        return carry

    lax.fori_loop(0, high_ref.shape[1] // CHUNK, body, 0)


def viscosity_kernel(field_ref, high_ref, low_ref, geom_ref, scale_ref, coef_ref, stack_ref):
    stack_ref[...] = stack_field(field_ref)
    viscosity_loop(
        stack_ref, high_ref, low_ref, geom_ref, scale_ref, coef_ref, field_ref.shape[1]
    )


def operate_kernel(
    field_ref, high_ref, low_ref, geom_ref, coef_ref, out_ref, stack_ref, total_ref
):
    stack_ref[...] = stack_field(field_ref)
    operate_loop(
        stack_ref, high_ref, low_ref, geom_ref, coef_ref, total_ref, field_ref.shape[1]
    )
    out_ref[0], out_ref[1] = unstack(total_ref[...])


def read_kernel(field_ref, high_ref, low_ref, wx_ref, wy_ref, read_ref, stack_ref):
    stack_ref[...] = stack_field(field_ref)
    read_loop(stack_ref, high_ref, low_ref, wx_ref, wy_ref, read_ref, field_ref.shape[1])


def spread_kernel(arrived_ref, high_ref, low_ref, wx_ref, wy_ref, out_ref, total_ref):
    spread_loop(arrived_ref, high_ref, low_ref, wx_ref, wy_ref, total_ref, out_ref.shape[1])
    out_ref[0], out_ref[1] = unstack(total_ref[...])


def call(kernel, out, scratch, *args):
    return pl.pallas_call(
        kernel,
        out_shape=jax.ShapeDtypeStruct(out, jnp.float32),
        in_specs=[pl.BlockSpec(memory_space=pltpu.VMEM)] * len(args),
        out_specs=pl.BlockSpec(memory_space=pltpu.VMEM),
        scratch_shapes=scratch,
        compiler_params=pltpu.CompilerParams(vmem_limit_bytes=48 * 1024 * 1024),
    )(*args)


def split_ids(ids, node_rows, columns):
    row = ids // (columns + 2)
    col = ids % (columns + 2)
    left, right = col == 0, col == columns + 1
    high = jnp.where(left | right, node_rows + 2, row)
    low = jnp.where(left, row, jnp.where(right, row + RIM, col - 1))
    return high, low


def weigh_rows(readings, precision, couple):
    grid_read = readings.reshape(-1, 128)
    grid_prec = precision.reshape(-1, 128)
    grid_couple = couple.reshape(-1, 128)
    column = jnp.arange(128)[None, :]
    next_prec = jnp.concatenate([grid_prec[:, 1:], grid_prec[:, :1]], axis=1)
    link_weight = jnp.where(column < 127, grid_couple * jnp.sqrt(grid_prec * next_prec), 0.0)
    zero_col = jnp.zeros_like(grid_read[:, :1])
    next_read = jnp.concatenate([grid_read[:, 1:], zero_col], axis=1)
    prev_read = jnp.concatenate([zero_col, grid_read[:, :-1]], axis=1)
    prev_link = jnp.concatenate([zero_col, link_weight[:, :-1]], axis=1)
    return (grid_prec * grid_read - link_weight * next_read - prev_link * prev_read).reshape(-1)


def ghosted(field):
    return padded(field, (("wide", 1), ("narrow", 2)), 1)


def reduce_rims(summed):
    side_cols = jnp.concatenate([summed[:, :, :1], summed[:, :, -1:]], axis=2)
    beside = padded(side_cols, (("narrow", 2),), 1)
    middle = summed[:, :, 1:-1]
    middle = middle.at[:, :, 0].add(beside[:, :, 0]).at[:, :, -1].add(beside[:, :, 3])
    side_rows = jnp.concatenate([middle[:, :1], middle[:, -1:]], axis=1)
    across = padded(side_rows, (("wide", 1),), 1)
    interior = middle[:, 1:-1]
    return interior.at[:, 0].add(across[:, 0]).at[:, -1].add(across[:, 3])


def norm_sum(residual):
    return lax.psum(jnp.sum(residual * residual), ("wide", "narrow"))


def per_device(
    state_vel,
    friction,
    basal_area,
    direction_beta,
    elem_nodes,
    elem_geom,
    elem_thick,
    live_blocks,
    pix_dest,
    pix_prec,
    pix_couple,
    obs_nodes,
    obs_bary,
    obs_angle,
):
    node_rows, columns = friction.shape
    rows = -(-(node_rows + 3) // 8) * 8
    elements = elem_nodes.shape[1]
    core_index = lax.axis_index("sub")
    alive = jnp.arange(elements, dtype=jnp.int32) // 128 < live_blocks[core_index]
    scale = jnp.where(alive, elem_thick * elem_geom[6], 0.0)[None, :]
    high, low = split_ids(elem_nodes, node_rows, columns)
    obs_high, obs_low = split_ids(obs_nodes, node_rows, columns)
    basal_drag = jnp.exp(friction) * basal_area
    stack = pltpu.VMEM((4 * rows, columns), jnp.bfloat16)
    total = pltpu.VMEM((4 * rows, columns), jnp.float32)

    def spread(field):
        wide = ghosted(field)
        room = ((0, 0), (0, RIM - node_rows - 2))
        rim = jnp.concatenate([jnp.pad(wide[:, :, 0], room), jnp.pad(wide[:, :, -1], room)], axis=1)
        gap = jnp.zeros((2, rows - node_rows - 3, columns), jnp.float32)
        return jnp.concatenate([wide[:, :, 1:-1], rim[:, None, :], gap], axis=1)

    def finish(partial):
        both = lax.psum(partial, "sub")
        rim = both[:, node_rows + 2]
        left = rim[:, : node_rows + 2, None]
        right = rim[:, RIM : RIM + node_rows + 2, None]
        return reduce_rims(jnp.concatenate([left, both[:, : node_rows + 2], right], axis=2))

    coefficient = call(
        viscosity_kernel, (1, elements), [stack], spread(state_vel), high, low, elem_geom, scale
    )

    def operate(field):
        partial = call(
            operate_kernel,
            (2, rows, columns),
            [stack, total],
            spread(field),
            high,
            low,
            elem_geom,
            coefficient,
        )
        return finish(partial) + basal_drag * field

    def solve_field(right_side):
        solution = jnp.zeros_like(right_side)
        residual = right_side
        direction = right_side
        norm_now = norm_sum(residual)
        for iteration in range(CG_ITERS):
            applied = operate(direction)
            step_size = norm_now / lax.psum(jnp.sum(direction * applied), ("wide", "narrow"))
            solution = solution + step_size * direction
            residual = residual - step_size * applied
            if iteration + 1 < CG_ITERS:
                norm_next = norm_sum(residual)
                direction = residual + norm_next / norm_now * direction
                norm_now = norm_next
        return solution

    owners = lax.axis_size(("wide", "narrow"))
    capacity = obs_angle.shape[0] // owners
    tangent_vel = solve_field(-basal_drag * direction_beta * state_vel)
    weight_x = obs_bary * jnp.cos(obs_angle)
    weight_y = obs_bary * jnp.sin(obs_angle)
    readings = call(
        read_kernel,
        (1, obs_angle.shape[0]),
        [stack],
        spread(tangent_vel),
        obs_high,
        obs_low,
        weight_x,
        weight_y,
    ).reshape(owners, capacity)
    returned = lax.all_to_all(readings, ("wide", "narrow"), split_axis=0, concat_axis=0, tiled=True)
    target = pix_dest[:, 0]
    onehot = (target[:, None] == jnp.arange(owners, dtype=jnp.int32)[None, :]).astype(jnp.int32)
    running = jnp.cumsum(onehot, axis=0, dtype=jnp.int32)
    slot_rank = jnp.sum(jnp.where(onehot == 1, running, 0), axis=1) - 1
    slot_index = target * capacity + slot_rank
    weighted = weigh_rows(returned.reshape(-1)[slot_index], pix_prec, pix_couple)
    outgoing = (
        jnp.zeros((owners * capacity,), jnp.float32)
        .at[slot_index]
        .set(weighted)
        .reshape(owners, capacity)
    )
    arrived = lax.all_to_all(outgoing, ("wide", "narrow"), split_axis=0, concat_axis=0, tiled=True)
    partial = call(
        spread_kernel,
        (2, rows, columns),
        [total],
        arrived.reshape(1, -1),
        obs_high,
        obs_low,
        weight_x,
        weight_y,
    )
    adjoint = solve_field(finish(partial))
    hess_vec = -basal_drag * (state_vel[0] * adjoint[0] + state_vel[1] * adjoint[1])
    return (tangent_vel, hess_vec)


def node_ids(ids, node_rows, columns):
    row = ids // (columns + 2)
    col = ids % (columns + 2)
    left, right = col == 0, col == columns + 1
    inner = jnp.where(row == 0, node_rows, jnp.where(row == node_rows + 1, row, row - 1))
    high = jnp.where(left | right, node_rows + 2, inner)
    low = jnp.where(left, row, jnp.where(right, row + RIM, col - 1))
    return high, low


SCALE = 12


def shared_chunk(stack_ref, work_ref, cols, rows):
    width = stack_ref.shape[1]
    ids = work_ref[0:6, cols].astype(jnp.int32)
    masks, onehots, value_x, value_y = [], [], [], []
    for a in range(3):
        masks.append(row_mask(ids[a : a + 1], rows))
        onehots.append(column_onehot(ids[3 + a : 4 + a], width))
        got_x, got_y = pick(stack_ref[...], masks[a], onehots[a])
        value_x.append(got_x)
        value_y.append(got_y)
    grad = [work_ref[6 + i : 7 + i, cols] for i in range(6)]
    return masks, onehots, grad, strain_rows((value_x, value_y), grad)


def shared_viscosity(stack_ref, work_ref, coef_ref, rows):
    def body(step, carry):
        cols = chunk_of(step)
        _, _, _, (exx, eyy, exy) = shared_chunk(stack_ref, work_ref, cols, rows)
        effective = exx * exx + eyy * eyy + exx * eyy + exy * exy + STRAIN_FLOOR
        viscosity = 0.5 * GLEN_B * jnp.exp(jnp.log(effective) * (-1.0 / 3.0))
        coef_ref[:, cols] = 2.0 * viscosity * work_ref[SCALE : SCALE + 1, cols]
        return carry

    lax.fori_loop(0, work_ref.shape[1] // CHUNK, body, 0, unroll=2)


def shared_operate(stack_ref, work_ref, coef_ref, total_ref, rows):
    total_ref[...] = jnp.zeros_like(total_ref)

    def body(step, carry):
        total = total_ref[...]
        parts = []
        for half in range(2):
            cols = chunk_of(2 * step + half)
            masks, onehots, grad, strain = shared_chunk(stack_ref, work_ref, cols, rows)
            exx, eyy, exy = strain
            coefficient = coef_ref[:, cols]
            sxx = coefficient * (2.0 * exx + eyy)
            syy = coefficient * (exx + 2.0 * eyy)
            sxy = coefficient * exy
            stacks = [
                masked_stack(
                    masks[a],
                    sxx * grad[a] + sxy * grad[3 + a],
                    syy * grad[3 + a] + sxy * grad[a],
                )
                for a in range(3)
            ]
            parts.append((stacks, onehots))
        for stacks, onehots in parts:
            total = total + add_in(stacks, onehots)
        total_ref[...] = total
        return carry

    lax.fori_loop(0, work_ref.shape[1] // (2 * CHUNK), body, 0)


SIDES = [(dw, dn) for dw in (-1, 0, 1) for dn in (-1, 0, 1)]
TILE = 8


def whole_kernel(
    wide,
    narrow,
    state_ref,
    friction_ref,
    area_ref,
    beta_ref,
    packed_ref,
    live_ref,
    dest_ref,
    prec_ref,
    couple_ref,
    obs_high_ref,
    obs_low_ref,
    wx_ref,
    wy_ref,
    tangent_ref,
    hess_ref,
    stack_ref,
    total_ref,
    coef_ref,
    drag_ref,
    vel_ref,
    p_ref,
    r_ref,
    x_ref,
    q_ref,
    field_send,
    field_recv,
    rim_send,
    rim_recv,
    sum_send,
    sum_recv,
    pix_send,
    pix_recv,
    other_ref,
    work_ref,
    other_sems,
    field_ss,
    field_rs,
    rim_ss,
    rim_rs,
    sum_ss,
    sum_rs,
    pix_ss,
    pix_rs,
):
    node_rows, columns = friction_ref.shape
    rows = vel_ref.shape[1]
    count = wide * narrow
    my_w = lax.axis_index("wide")
    my_n = lax.axis_index("narrow")
    my_s = lax.axis_index("sub")
    me = my_w * narrow + my_n
    f32 = jnp.float32

    def place_of(q):
        return {"wide": q // narrow, "narrow": lax.rem(q, narrow), "sub": my_s}

    partner = {"wide": my_w, "narrow": my_n, "sub": 1 - my_s}
    barrier = pltpu.get_barrier_semaphore()
    pl.semaphore_signal(barrier, inc=1, device_id=partner, device_id_type=pl.DeviceIdType.MESH)
    for k in range(1, count):
        pl.semaphore_signal(
            barrier,
            inc=1,
            device_id=place_of(lax.rem(me + k, count)),
            device_id_type=pl.DeviceIdType.MESH,
        )
    pl.semaphore_wait(barrier, count)

    trade = pltpu.make_async_remote_copy(
        src_ref=packed_ref,
        dst_ref=other_ref,
        send_sem=other_sems.at[0],
        recv_sem=other_sems.at[1],
        device_id=partner,
        device_id_type=pl.DeviceIdType.MESH,
    )
    trade.start()
    row_at = lax.broadcasted_iota(jnp.int32, (rows, columns), 0)
    lane_at = lax.broadcasted_iota(jnp.int32, (rows, columns), 1)
    eye_row = lax.broadcasted_iota(jnp.int32, (rows, RIM), 0)
    eye_lane = lax.broadcasted_iota(jnp.int32, (rows, RIM), 1)
    eye_row = jnp.where(
        eye_row < node_rows,
        eye_row + 1,
        jnp.where(eye_row == node_rows, 0, jnp.where(eye_row == node_rows + 1, eye_row, -1)),
    )
    eye = eye_row == eye_lane
    rim_lane = lax.broadcasted_iota(jnp.int32, (1, RIM), 1)

    def exists(dw, dn):
        w, n = my_w + dw, my_n + dn
        return (w >= 0) & (w < wide) & (n >= 0) & (n < narrow)

    has_up, has_down = my_w > 0, my_w < wide - 1
    has_left, has_right = my_n > 0, my_n < narrow - 1
    rim_row = jnp.where(lane_at >= RIM, lane_at - RIM, lane_at)
    rim_side = ((lane_at < RIM) & has_left) | ((lane_at >= RIM) & has_right)
    rim_in = (
        ((rim_row >= 1) & (rim_row <= node_rows))
        | ((rim_row == 0) & has_up)
        | ((rim_row == node_rows + 1) & has_down)
    )
    inside = (
        (row_at < node_rows)
        | ((row_at == node_rows) & has_up)
        | ((row_at == node_rows + 1) & has_down)
        | ((row_at == node_rows + 2) & rim_side & rim_in)
    )

    def col_lanes(field, lane):
        column = field[:, lane : lane + 1]
        return jnp.sum(jnp.where(eye, column, 0.0), axis=0, keepdims=True)

    def lanes_col(lanes):
        return jnp.sum(jnp.where(eye, lanes, 0.0), axis=1, keepdims=True)

    def rim_copy(k, slot):
        dw, dn = SIDES[slot]
        return pltpu.make_async_remote_copy(
            src_ref=rim_send.at[k],
            dst_ref=rim_recv.at[k, 8 - slot],
            send_sem=rim_ss.at[k, slot],
            recv_sem=rim_rs.at[k, 8 - slot],
            device_id={"wide": my_w + dw, "narrow": my_n + dn, "sub": my_s},
            device_id_type=pl.DeviceIdType.MESH,
        )

    def rim_landed(k, slot):
        dw, dn = SIDES[slot]
        return pltpu.make_async_remote_copy(
            src_ref=rim_send.at[k],
            dst_ref=rim_recv.at[k, slot],
            send_sem=rim_ss.at[k, slot],
            recv_sem=rim_rs.at[k, slot],
            device_id={"wide": my_w + dw, "narrow": my_n + dn, "sub": my_s},
            device_id_type=pl.DeviceIdType.MESH,
        )

    def rim_start(k, fields):
        lines = []
        for at in (node_rows, 0, node_rows - 1, node_rows + 1, node_rows + 2):
            lines += [field[at : at + 1] for field in fields]
        lines += [
            jnp.concatenate([col_lanes(field, 0), col_lanes(field, columns - 1)], axis=1)
            for field in fields
        ]
        for i, line in enumerate(lines):
            rim_send[k, i : i + 1, :] = line
        for slot, side in enumerate(SIDES):
            if side != (0, 0):

                @pl.when(exists(*side))
                def _():
                    rim_copy(k, slot).start()

    def moved(lanes, dw):
        if dw == 0:
            return lanes
        if dw < 0:
            turned = pltpu.roll(lanes, (RIM - node_rows) % RIM, 1)
            return jnp.where(rim_lane < 2, turned, 0.0)
        turned = pltpu.roll(lanes, node_rows, 1)
        keep = (rim_lane == node_rows) | (rim_lane == node_rows + 1)
        return jnp.where(keep, turned, 0.0)

    def rim_finish(k, fields):
        for slot, side in enumerate(SIDES):
            if side != (0, 0):

                @pl.when(exists(*side))
                def _():
                    rim_landed(k, slot).wait_recv()
                    rim_landed(k, slot).wait_send()

        done = []
        for c, field in enumerate(fields):

            def got(dw, dn, line, low, size):
                slot = SIDES.index((dw, dn))
                at = 2 * line + c
                value = rim_recv[k, slot, at : at + 1, low : low + size]
                return jnp.where(exists(dw, dn), value, 0.0)

            left_rim = jnp.zeros((1, RIM), f32)
            right_rim = jnp.zeros((1, RIM), f32)
            left_col = jnp.zeros((1, RIM), f32)
            right_col = jnp.zeros((1, RIM), f32)
            for dw in (-1, 1):
                left_rim = left_rim + moved(got(dw, 0, 4, 0, RIM), dw)
                right_rim = right_rim + moved(got(dw, 0, 4, RIM, RIM), dw)
            for dw in (0, -1, 1):
                left_col = left_col + moved(got(dw, -1, 4, RIM, RIM), dw)
                left_rim = left_rim + moved(got(dw, -1, 5, RIM, RIM), dw)
                right_col = right_col + moved(got(dw, 1, 4, 0, RIM), dw)
                right_rim = right_rim + moved(got(dw, 1, 5, 0, RIM), dw)
            result = field
            for at, dw, line in (
                (node_rows, -1, 2),
                (0, -1, 3),
                (node_rows - 1, 1, 0),
                (node_rows + 1, 1, 1),
            ):
                result = result + jnp.where(row_at == at, got(dw, 0, line, 0, columns), 0.0)
            rim = jnp.concatenate([left_rim, right_rim], axis=1)
            result = result + jnp.where(row_at == node_rows + 2, rim, 0.0)
            result = result + jnp.where(lane_at == 0, lanes_col(left_col), 0.0)
            result = result + jnp.where(lane_at == columns - 1, lanes_col(right_col), 0.0)
            done.append(jnp.where(inside, result, 0.0))
        return done

    def all_copy(send, recv, ss, rs, k, target, slot):
        return pltpu.make_async_remote_copy(
            src_ref=send,
            dst_ref=recv.at[k, slot],
            send_sem=ss.at[k, target],
            recv_sem=rs.at[k, slot],
            device_id=place_of(target),
            device_id_type=pl.DeviceIdType.MESH,
        )

    def sum_start(k, *values):
        for i, value in enumerate(values):
            sum_send[k, i : i + 1, :] = jnp.broadcast_to(value, (1, 128))
        for j in range(1, count):
            q = lax.rem(me + j, count)
            all_copy(sum_send.at[k], sum_recv, sum_ss, sum_rs, k, q, me).start()
        sum_recv[k, me] = sum_send[k]

    def sum_finish(k):
        for j in range(1, count):
            q = lax.rem(me + j, count)
            copy = all_copy(sum_send.at[k], sum_recv, sum_ss, sum_rs, k, q, q)
            copy.wait_recv()
            copy.wait_send()
        total = sum_recv[k, 0]
        for q in range(1, count):
            total = total + sum_recv[k, q]
        return total[0:1, 0:1], total[1:2, 0:1]

    def pix_start(k):
        for j in range(1, count):
            q = lax.rem(me + j, count)
            all_copy(pix_send.at[k, q], pix_recv, pix_ss, pix_rs, k, q, me).start()
        pix_recv[k, me] = pix_send[k, me]

    def pix_finish(k):
        for j in range(1, count):
            q = lax.rem(me + j, count)
            copy = all_copy(pix_send.at[k, q], pix_recv, pix_ss, pix_rs, k, q, q)
            copy.wait_recv()
            copy.wait_send()

    def core_start(k):
        field_send[k, 0], field_send[k, 1] = unstack(total_ref[...])
        copy = pltpu.make_async_remote_copy(
            src_ref=field_send.at[k],
            dst_ref=field_recv.at[k],
            send_sem=field_ss.at[k],
            recv_sem=field_rs.at[k],
            device_id=partner,
            device_id_type=pl.DeviceIdType.MESH,
        )
        copy.start()
        return copy

    def core_finish(k, copy):
        copy.wait()
        return [field_send[k, c] + field_recv[k, c] for c in range(2)]

    def dot(a, b):
        down = jnp.sum(a * b, axis=0, keepdims=True)
        return jnp.sum(down, axis=1, keepdims=True)

    def both(a_ref, b_ref, size):
        return dot(a_ref[0, :size], b_ref[0, :size]) + dot(a_ref[1, :size], b_ref[1, :size])

    def solve(field_at, rim_at, sum_at):
        for c in range(2):
            p_ref[c] = r_ref[c]
        norm_now = None
        for step in range(CG_ITERS):
            stack_ref[...] = stack_field(p_ref)
            shared_operate(stack_ref, work_ref, coef_ref, total_ref, rows)
            copy = core_start(field_at + step)
            norm = both(r_ref, r_ref, node_rows)
            energy = jnp.zeros((1, 1), f32)
            for c in range(2):
                field = p_ref[c, :node_rows]
                energy = energy + dot(drag_ref[:node_rows] * field, field)
            local = core_finish(field_at + step, copy)
            rim_start(rim_at + step, local)
            energy = energy + dot(local[0], p_ref[0]) + dot(local[1], p_ref[1])
            sum_start(sum_at + 2 * step, norm, energy)
            applied = rim_finish(rim_at + step, local)
            for c in range(2):
                q_ref[c] = applied[c] + drag_ref[...] * p_ref[c]
            norm_now, energy = sum_finish(sum_at + 2 * step)
            alpha = norm_now / energy
            if step + 1 < CG_ITERS:
                for c in range(2):
                    r_ref[c] = r_ref[c] - alpha * q_ref[c]
                norm = both(r_ref, r_ref, node_rows)
                sum_start(sum_at + 2 * step + 1, norm)
            for c in range(2):
                if step == 0:
                    x_ref[c] = alpha * p_ref[c]
                else:
                    x_ref[c] = x_ref[c] + alpha * p_ref[c]
            if step + 1 < CG_ITERS:
                norm_next, _ = sum_finish(sum_at + 2 * step + 1)
                ratio = norm_next / norm_now
                for c in range(2):
                    p_ref[c] = r_ref[c] + ratio * p_ref[c]

    sum_send[...] = jnp.zeros_like(sum_send)
    rim_send[...] = jnp.zeros_like(rim_send)
    pix_send[...] = jnp.zeros_like(pix_send)
    gap = jnp.zeros((rows - node_rows, columns), f32)

    def grown(value):
        return jnp.concatenate([value, gap], axis=0)

    vel = [grown(state_ref[0]), grown(state_ref[1])]
    rim_start(0, vel)
    other = [grown(jnp.exp(friction_ref[...]) * area_ref[...]), grown(beta_ref[...])]
    rim_start(1, other)
    vel_ref[0], vel_ref[1] = rim_finish(0, vel)
    drag, beta = rim_finish(1, other)
    drag_ref[...] = drag
    for c in range(2):
        r_ref[c] = -drag * beta * vel_ref[c]
    stack_ref[...] = stack_field(vel_ref)
    trade.wait()
    share = work_ref.shape[1] // 128
    blocks = packed_ref.shape[0]
    first_live = live_ref[0]
    all_live = first_live + live_ref[1]

    def take(i, carry):
        position = my_s * share + i
        of_first = position < first_live
        at = jnp.where(
            of_first, jnp.minimum(position, blocks - 1), jnp.clip(position - first_live, 0, blocks - 1)
        )
        mine = jnp.where(of_first, 1, 0) + my_s == 1
        block = jnp.where(mine, packed_ref[at], other_ref[at])
        alive = (position < all_live) | (piece_row < SCALE)
        cols = pl.ds(pl.multiple_of(i * 128, 128), 128)
        work_ref[:, cols] = jnp.where(alive, block, 0.0)
        return carry

    piece_row = lax.broadcasted_iota(jnp.int32, (16, 128), 0)
    lax.fori_loop(0, share, take, 0)
    shared_viscosity(stack_ref, work_ref, coef_ref, rows)
    solve(0, 2, 0)
    tangent_ref[...] = x_ref[:, :node_rows]

    capacity = obs_high_ref.shape[1] // count
    lines = capacity // 128
    stack_ref[...] = stack_field(x_ref)

    def read(step, carry):
        cols = pl.ds(pl.multiple_of(step * capacity, 128), capacity)
        _, _, values = gather_chunk(
            stack_ref[...], obs_high_ref, obs_low_ref, cols, rows, columns
        )
        total = jnp.zeros((1, capacity), f32)
        for a in range(3):
            total = total + (
                wx_ref[a : a + 1, cols] * values[0][a] + wy_ref[a : a + 1, cols] * values[1][a]
            )
        for j in range(lines):
            pix_send[0, step, j : j + 1, :] = total[:, j * 128 : (j + 1) * 128]
        return carry

    lax.fori_loop(0, count, read, 0, unroll=2)
    pix_start(0)

    dest = dest_ref[...]
    pixel_rows = dest.shape[0]
    named = jnp.concatenate(
        [jnp.where(dest == q, 1.0, 0.0) for q in range(count)], axis=0
    ).astype(jnp.bfloat16)
    first = lax.broadcasted_iota(jnp.int32, (128, 128), 0)
    second = lax.broadcasted_iota(jnp.int32, (128, 128), 1)
    before = jnp.where(first < second, 1.0, 0.0).astype(jnp.bfloat16)
    ones = jnp.ones((128, 128), jnp.bfloat16)
    within = jnp.dot(named, before, preferred_element_type=f32)
    per_row = jnp.dot(named, ones, preferred_element_type=f32).astype(jnp.bfloat16)
    size = count * pixel_rows
    first = lax.broadcasted_iota(jnp.int32, (size, size), 0)
    second = lax.broadcasted_iota(jnp.int32, (size, size), 1)
    start = first // pixel_rows * pixel_rows
    above = jnp.where((second >= start) & (second < first), 1.0, 0.0).astype(jnp.bfloat16)
    ranks = within + jnp.dot(above, per_row, preferred_element_type=f32)
    rank = jnp.zeros((pixel_rows, 128), f32)
    for q in range(count):
        rank = rank + jnp.where(dest == q, ranks[q * pixel_rows : (q + 1) * pixel_rows], 0.0)
    rank = rank.astype(jnp.int32)
    slot_line = dest * TILE + rank // 128
    slot_lane = lax.rem(rank, 128)

    def flat(value):
        return jnp.concatenate([value[i : i + 1] for i in range(pixel_rows)], axis=1)

    table = count * TILE
    line_mask = row_mask(flat(slot_line), table)
    lane_hot = column_onehot(flat(slot_lane), 128)
    pix_finish(0)
    high, low = split_pair(pix_recv[0].reshape(table, 128))
    spread_out = jnp.dot(
        jnp.concatenate([high, low], axis=0), lane_hot, preferred_element_type=f32
    )
    spread_out = spread_out[:table] + spread_out[table:]
    line = jnp.sum(jnp.where(line_mask, spread_out, 0.0), axis=0, keepdims=True)
    reading = jnp.concatenate(
        [line[:, i * 128 : (i + 1) * 128] for i in range(pixel_rows)], axis=0
    )
    precision = prec_ref[...]
    column = lax.broadcasted_iota(jnp.int32, (pixel_rows, 128), 1)
    link = jnp.where(
        column < 127,
        couple_ref[...] * jnp.sqrt(precision * pltpu.roll(precision, 127, 1)),
        0.0,
    )
    weighted = (
        precision * reading
        - link * pltpu.roll(reading, 127, 1)
        - pltpu.roll(link, 1, 1) * pltpu.roll(reading, 1, 1)
    )
    weighted = flat(weighted)
    top = weighted.astype(jnp.bfloat16).astype(f32)
    left = jnp.concatenate(
        [jnp.where(line_mask, part, 0.0).astype(jnp.bfloat16) for part in (top, weighted - top)],
        axis=0,
    )
    out = lax.dot_general(
        left, lane_hot, (((1,), (1,)), ((), ())), preferred_element_type=f32
    )
    pix_send[1] = (out[:table] + out[table:]).reshape(count, TILE, 128)
    pix_start(1)
    pix_finish(1)

    total_ref[...] = jnp.zeros_like(total_ref)

    def scatter(step, carry):
        cols = pl.ds(pl.multiple_of(step * capacity, 128), capacity)
        tile = pix_recv[1, step]
        arrived = jnp.concatenate([tile[j : j + 1] for j in range(lines)], axis=1)
        stacks, onehots = [], []
        for a in range(3):
            mask = row_mask(obs_high_ref[a : a + 1, cols], rows)
            onehots.append(column_onehot(obs_low_ref[a : a + 1, cols], columns))
            stacks.append(
                masked_stack(
                    mask, arrived * wx_ref[a : a + 1, cols], arrived * wy_ref[a : a + 1, cols]
                )
            )
        total_ref[...] += add_in(stacks, onehots)
        return carry

    lax.fori_loop(0, count, scatter, 0, unroll=2)
    local = core_finish(2, core_start(2))
    rim_start(4, local)
    r_ref[0], r_ref[1] = rim_finish(4, local)
    solve(3, 5, 3)
    hess_ref[...] = -drag_ref[:node_rows] * (
        state_ref[0] * x_ref[0, :node_rows] + state_ref[1] * x_ref[1, :node_rows]
    )


def fused_device(
    state_vel,
    friction,
    basal_area,
    direction_beta,
    elem_nodes,
    elem_geom,
    elem_thick,
    live_blocks,
    pix_dest,
    pix_prec,
    pix_couple,
    obs_nodes,
    obs_bary,
    obs_angle,
):
    node_rows, columns = friction.shape
    rows = -(-(node_rows + 3) // 8) * 8
    elements = elem_nodes.shape[1]
    wide, narrow = lax.axis_size("wide"), lax.axis_size("narrow")
    count = wide * narrow
    alive = jnp.arange(elements, dtype=jnp.int32) // 128 < live_blocks[lax.axis_index("sub")]
    scale = jnp.where(alive, elem_thick * elem_geom[6], 0.0)[None, :]
    high, low = node_ids(elem_nodes, node_rows, columns)
    packed = jnp.concatenate(
        [
            high.astype(jnp.float32),
            low.astype(jnp.float32),
            elem_geom[0:6],
            scale,
            jnp.zeros((3, elements), jnp.float32),
        ],
        axis=0,
    )
    packed = packed.reshape(16, -1, 128).transpose(1, 0, 2)
    share = 2 * (elements // 128) // 3
    obs_high, obs_low = node_ids(obs_nodes, node_rows, columns)
    weight_x = obs_bary * jnp.cos(obs_angle)
    weight_y = obs_bary * jnp.sin(obs_angle)
    f32 = jnp.float32
    pair = pltpu.VMEM((2, rows, columns), f32)
    args = (
        state_vel,
        friction,
        basal_area,
        direction_beta,
        packed,
        live_blocks,
        pix_dest.reshape(-1, 128),
        pix_prec.reshape(-1, 128),
        pix_couple.reshape(-1, 128),
        obs_high,
        obs_low,
        weight_x,
        weight_y,
    )
    dma = pltpu.SemaphoreType.DMA
    return pl.pallas_call(
        functools.partial(whole_kernel, wide, narrow),
        out_shape=(
            jax.ShapeDtypeStruct((2, node_rows, columns), f32),
            jax.ShapeDtypeStruct((node_rows, columns), f32),
        ),
        in_specs=[
            pl.BlockSpec(memory_space=pltpu.SMEM if arg is live_blocks else pltpu.VMEM)
            for arg in args
        ],
        out_specs=(pl.BlockSpec(memory_space=pltpu.VMEM),) * 2,
        scratch_shapes=[
            pltpu.VMEM((4 * rows, columns), jnp.bfloat16),
            pltpu.VMEM((4 * rows, columns), f32),
            pltpu.VMEM((1, share * 128), f32),
            pltpu.VMEM((rows, columns), f32),
            pair,
            pair,
            pair,
            pair,
            pair,
            pltpu.VMEM((5, 2, rows, columns), f32),
            pltpu.VMEM((5, 2, rows, columns), f32),
            pltpu.VMEM((7, 16, columns), f32),
            pltpu.VMEM((7, 9, 16, columns), f32),
            pltpu.VMEM((6, 8, 128), f32),
            pltpu.VMEM((6, count, 8, 128), f32),
            pltpu.VMEM((2, count, TILE, 128), f32),
            pltpu.VMEM((2, count, TILE, 128), f32),
            pltpu.VMEM(packed.shape, f32),
            pltpu.VMEM((16, share * 128), f32),
            dma((2,)),
            dma((5,)),
            dma((5,)),
            dma((7, 9)),
            dma((7, 9)),
            dma((6, count)),
            dma((6, count)),
            dma((2, count)),
            dma((2, count)),
        ],
        compiler_params=pltpu.CompilerParams(
            collective_id=0, has_side_effects=True, vmem_limit_bytes=48 * 1024 * 1024
        ),
    )(*args)


def choose(*args):
    count = lax.axis_size("wide") * lax.axis_size("narrow")
    capacity = args[-1].shape[0] // count
    columns = args[1].shape[1]
    share = 2 * (args[4].shape[1] // 128) // 3
    fits = share * 128 % (2 * CHUNK) == 0 and count % 2 == 0
    if fits and capacity % 128 == 0 and capacity <= 128 * TILE and columns == 2 * RIM and args[1].shape[0] + 2 <= RIM:
        return fused_device(*args)
    return per_device(*args)


def solution(mesh):
    placed = (
        P(None, ("groups", "wide"), "narrow"),
        P(("groups", "wide"), "narrow"),
        P(("groups", "wide"), "narrow"),
        P(("groups", "wide"), "narrow"),
        P(None, ("groups", "wide", "narrow", "sub")),
        P(None, ("groups", "wide", "narrow", "sub")),
        P(("groups", "wide", "narrow", "sub")),
        P(("groups", "wide", "narrow")),
        P(("groups", "wide", "narrow", "sub"), None),
        P(("groups", "wide", "narrow", "sub")),
        P(("groups", "wide", "narrow", "sub")),
        P(None, ("groups", "wide", "narrow", "sub")),
        P(None, ("groups", "wide", "narrow", "sub")),
        P(("groups", "wide", "narrow", "sub")),
    )
    return jax.shard_map(
        choose,
        mesh=mesh,
        in_specs=placed,
        out_specs=(P(None, ("groups", "wide"), "narrow"), P(("groups", "wide"), "narrow")),
        check_vma=False,
    )
```
